512 devices in a mesh: dp: 32 (over z, y_hi), tensor: 16 (over x, y_lo, core).
Axes of the slice: x: 4, y: 8 (y_hi: 4, y_lo: 2; y = y_hi * 2 + y_lo), z: 8, core: 2. Of those that a mesh axis runs over, the one named last changes fastest.
Arguments:
- hidden: bfloat16 [4096, 8192], P('dp', 'tensor'), may hold values from -27 to 27
- gain: bfloat16 [8192], P('tensor'), may hold values from 0.5 to 1.5
- proj_weight: bfloat16 [8192, 4096], P('dp', 'tensor'), may hold values from -0.0625 to 0.0625
- b_c: bfloat16 [4096, 4096], P('dp', 'tensor'), may hold values from -4 to 4
- ssm_x: bfloat16 [4096, 16384], P('dp', 'tensor'), may hold values from -4 to 4
- dy: bfloat16 [4096, 16384], P('dp', 'tensor'), may hold values from -0.015625 to 0.015625
- log_decay: float32 [4096, 256], P('dp', 'tensor'), may hold values from -0.75 to 0
Outputs:
- input_grad: bfloat16 [4096, 8192], P('dp', 'tensor')
- weight_grad: bfloat16 [8192, 4096], P('dp', 'tensor')
The draws below stay inside these ranges and needn't reach their ends.
All inputs are finite; a program needn't handle non-finite values.
Results may differ from the reference program's by a relative error of at most 0.025.
Values may be sent and summed in bfloat16 or wider, within the bound.
A program may use at most 64 MiB of HBM per device.

```python
import math
import jax
import jax.numpy as jnp
from jax import lax

D = 8192
STATE = 256
MHEAD = 64
TOKENS_PER_SHARD = 128
GROUPS = 8
MHEADS = 256
GROUP_HEADS = 32
COLS = 4096
TOKEN_TOTAL = 4096
N_DP = 32
N_TENSOR = 16


def draw_hidden(key, part):
    key = jax.random.fold_in(key, 13)
    row_key, col_key, core_key = jax.random.split(key, 3)
    row_scale = jnp.exp(jax.random.uniform(row_key, (TOKEN_TOTAL, 1), jnp.float32, 0.0, math.log(10.0)))
    col_scale = jnp.exp(jax.random.uniform(col_key, (1, D), jnp.float32, 0.0, math.log(3.0)))
    core = jnp.clip(jax.random.normal(core_key, (TOKEN_TOTAL, D), jnp.float32), -3.0, 3.0)
    return (core * row_scale * col_scale * 0.3).astype(jnp.bfloat16)


def draw_log_decay(key, part):
    key = jax.random.fold_in(key, 14)
    speed_random_key, wobble_random_key, spike_random_key, depth_random_key = jax.random.split(key, 4)
    lowest = math.log(0.5 / TOKENS_PER_SHARD)
    highest = math.log(0.03)
    speed_factors = jnp.exp(jax.random.uniform(speed_random_key, (1, MHEADS), jnp.float32, lowest, highest))
    random_wobble = jax.random.uniform(wobble_random_key, (TOKEN_TOTAL, MHEADS), jnp.float32, 0.5, 1.5)
    spike_position = jax.random.bernoulli(spike_random_key, 3.0 / TOKENS_PER_SHARD, (TOKEN_TOTAL, 1))
    spike_events = jnp.where(spike_position, jax.random.uniform(depth_random_key, (TOKEN_TOTAL, 1), jnp.float32, 0.22, 0.6), 0.0)
    return -(speed_factors * random_wobble + spike_events)


def steps_of(key, dims, cuts, smallest, largest):
    factor_of = 1.0
    for position, blocks in cuts:
        steps = jax.random.uniform(jax.random.fold_in(jax.random.fold_in(key, 6), position), (blocks,), jnp.float32, smallest / len(cuts), largest / len(cuts))
        factor_of = factor_of * jnp.repeat(jnp.exp(steps), dims[position] // blocks).reshape((-1,) + (1,) * (len(dims) - 1 - position))
    return factor_of


def normal_values(own_key, dims, scale, most, shards=(), kind=jnp.bfloat16):
    values = jax.random.normal(own_key, dims, jnp.float32) * scale
    if len(shards) > 0:
        values = steps_of(own_key, dims, shards, -0.22, 0.18) * values
    return jnp.clip(values, min=-most, max=most).astype(kind)


def setup_inputs(seed: int = 0) -> dict:
    keys = jax.random.split(jax.random.key(seed), 8)
    hidden = draw_hidden(jax.random.fold_in(keys[7], 71), 0)
    gain = jnp.clip(1.0 + 0.1 * jax.random.normal(keys[1], (D,), jnp.float32), 0.5, 1.5).astype(jnp.bfloat16)
    proj_weight = normal_values(keys[2], (D, COLS), D ** -0.5, 0.0625, ((0, 32), (1, 16)))
    b_c = normal_values(keys[3], (TOKEN_TOTAL, COLS), 1.0, 4.0, ((0, 32), (1, 16)))
    ssm_x = normal_values(keys[4], (TOKEN_TOTAL, MHEADS * MHEAD), 1.0, 4.0, ((0, 32), (1, 16)))
    dy = normal_values(keys[5], (TOKEN_TOTAL, MHEADS * MHEAD), (2.0 / (MHEAD * GROUP_HEADS * TOKENS_PER_SHARD) ** 0.5), 0.015625, ((0, 32), (1, 16)))
    log_decay = draw_log_decay(jax.random.fold_in(keys[7], 71), 0)
    return dict(hidden=hidden, gain=gain, proj_weight=proj_weight, b_c=b_c, ssm_x=ssm_x, dy=dy, log_decay=log_decay)


EPSILON = 1e-05

def round_low(value):
    return lax.optimization_barrier(value.astype(jnp.bfloat16)).astype(jnp.float32)

def causal_mask(length):
    return jnp.arange(length)[:, None] >= jnp.arange(length)[None, :]

def mamba_grads(bc_seq, input_seq, grad_seq, decay_seq):
    length = input_seq.shape[0]
    input_f = input_seq.astype(jnp.float32).reshape(length, MHEADS, MHEAD)
    grad_f = grad_seq.astype(jnp.float32).reshape(length, MHEADS, MHEAD)
    inner_prod = jnp.einsum('thd,shd->hts', grad_f, input_f)
    running = jnp.cumsum(decay_seq, axis=0).T
    log_gap = running[:, :, None] - running[:, None, :]
    decays = jnp.exp(jnp.where(causal_mask(length)[None], log_gap, -jnp.inf))
    dgram = (inner_prod * decays).reshape(GROUPS, GROUP_HEADS, length, length).sum(axis=1)
    bc_f = bc_seq.astype(jnp.float32).reshape(length, GROUPS, 2, 2, STATE // 2)
    b_proj = bc_f[:, :, :, 0].reshape(length, GROUPS, STATE)
    c_proj = bc_f[:, :, :, 1].reshape(length, GROUPS, STATE)
    grad_c = jnp.einsum('gts,sgn->tgn', dgram, b_proj, precision=lax.Precision.HIGHEST)
    grad_b = jnp.einsum('gts,tgn->sgn', dgram, c_proj, precision=lax.Precision.HIGHEST)
    stacked = jnp.stack([grad_b.reshape(length, GROUPS, 2, STATE // 2), grad_c.reshape(length, GROUPS, 2, STATE // 2)], axis=3)
    return stacked.reshape(length, COLS).astype(jnp.bfloat16)

def reference(hidden, gain, proj_weight, b_c, ssm_x, dy, log_decay):

    def by_sequence(array):
        return array.reshape((N_DP, TOKENS_PER_SHARD) + array.shape[1:])

    def per_sequence(seq_items):
        bc_seq, input_seq, grad_seq, decay_seq = seq_items
        return mamba_grads(bc_seq, input_seq, grad_seq, decay_seq)
    dproj = lax.map(per_sequence, tuple((by_sequence(array) for array in (b_c, ssm_x, dy, log_decay))))
    hidden_f = hidden.astype(jnp.float32)
    root_mean = jnp.sqrt(lax.optimization_barrier(jnp.mean(hidden_f * hidden_f, axis=-1, keepdims=True)) + EPSILON)
    unit_rows = hidden_f / root_mean
    gain_f = gain.astype(jnp.float32)
    normed = (unit_rows * gain_f).astype(jnp.bfloat16)
    inv_root = 1.0 / math.sqrt(TOKEN_TOTAL)

    def add_sequence(running_sum, seq_items):
        normed_seq, grad_seq = seq_items
        block_term = jnp.dot(normed_seq.T, grad_seq, preferred_element_type=jnp.float32) * inv_root
        return (running_sum + round_low(block_term), None)
    weight_sum, _ = lax.scan(add_sequence, jnp.zeros((D, COLS), jnp.float32), (by_sequence(normed), dproj))
    weight_grad = weight_sum.astype(jnp.bfloat16)
    grad_blocks = dproj.reshape(TOKEN_TOTAL, N_TENSOR, STATE).transpose(1, 0, 2)
    weight_blocks = proj_weight.reshape(D, N_TENSOR, STATE).transpose(1, 0, 2)

    def add_block(running_sum, block_items):
        grad_block, weight_block = block_items
        block_term = jnp.dot(grad_block, weight_block.T, preferred_element_type=jnp.float32)
        return (running_sum + round_low(block_term), None)
    dnormed, _ = lax.scan(add_block, jnp.zeros((TOKEN_TOTAL, D), jnp.float32), (grad_blocks, weight_blocks))
    scaled = gain_f * dnormed
    mean_term = lax.optimization_barrier(jnp.mean(scaled * unit_rows, axis=-1, keepdims=True))
    input_grad = ((scaled - unit_rows * mean_term) / root_mean).astype(jnp.bfloat16)
    return (input_grad, weight_grad)
```

```python
import jax
import jax.numpy as jnp
from jax import lax
from jax.experimental import pallas as pl
from jax.experimental.pallas import tpu as pltpu
from jax.sharding import PartitionSpec as P

MHEAD = 64
EPSILON = 1e-05
MESH = pl.DeviceIdType.MESH
F32 = jnp.float32
BF16 = jnp.bfloat16
HIGHEST = lax.Precision.HIGHEST


def device(za, zb, yh, x, yl, c):
    return {"dp": (za * 2 + zb) * 4 + yh, "tensor": x * 4 + yl * 2 + c}


def nt_dot(a, b, precision=None):
    return lax.dot_general(
        a, b, (((1,), (1,)), ((), ())), preferred_element_type=F32, precision=precision
    )


def nn_dot(a, b, precision=None):
    return lax.dot_general(
        a, b, (((1,), (0,)), ((), ())), preferred_element_type=F32, precision=precision
    )


class Slots:
    def __init__(self):
        self.count = 0

    def take(self, n):
        first = self.count
        self.count += n
        return first


SLOTS = Slots()
S_HID = SLOTS.take(4)
S_HAG = SLOTS.take(8)
S_W = SLOTS.take(8)
S_SQ = SLOTS.take(9)
S_GRAM = SLOTS.take(1)
S_DY = SLOTS.take(4)
S_DZ = SLOTS.take(4)
S_DC = SLOTS.take(8)
S_P = SLOTS.take(8)
S_Q = SLOTS.take(4)
S_G = SLOTS.take(8)
S_MEAN = SLOTS.take(9)
N_SLOTS = SLOTS.count


def kernel(
    hid_ref,
    gain_ref,
    w_ref,
    bc_ref,
    x_ref,
    dy_ref,
    ld_ref,
    igrad_ref,
    wgrad_ref,
    ht,
    hall,
    wall,
    sums,
    sums_in,
    gram,
    dall,
    psend,
    precv,
    rsum,
    qrecv,
    gsend,
    grecv,
    ssem,
    rsem,
    lsem,
):
    dp = lax.axis_index("dp")
    ten = lax.axis_index("tensor")
    z, yh = dp // 4, dp % 4
    za, zb = z // 2, z % 2
    x, yl, c = ten // 4, (ten // 2) % 2, ten % 2
    me = (za, zb, yh, x, yl, c)

    def remote(src, dst, slot, dev, rslot=None):
        rslot = slot if rslot is None else rslot
        return pltpu.make_async_remote_copy(
            src_ref=src,
            dst_ref=dst,
            send_sem=ssem.at[slot],
            recv_sem=rsem.at[rslot],
            device_id=device(*dev),
            device_id_type=MESH,
        )

    sibling = (za, zb, yh, x, yl, 1 - c)
    plane = [(dx, fy) for dx in range(4) for fy in range(2) if dx or fy]
    plane.sort(key=lambda o: (o[0] == 2, o[0] != 0))

    def plane_dev(dx, fy):
        return (za, zb, yh, (x + dx) % 4, (yl + fy) % 2, c)

    def plane_src(dx, fy):
        return (x + 4 - dx) % 4, (yl + fy) % 2

    def far(dza, fc):
        return ((za + dza) % 4, zb, yh, x, yl, (c + fc) % 2)

    depth = [(dza, fc) for dza in (2, 1, 3) for fc in range(2)] + [(0, 1)]

    def hid_target(i, h):
        return (za, yl, 2 * c + i, x, zb, h)

    def hid_target_is_me(i, h):
        return (yl == zb) & (yh == 2 * c + i) & (c == h)

    def hid_source(ys):
        return (za, yl, ys, x, zb, yh // 2)

    def hid_source_is_me(ys):
        return (yl == zb) & (ys == yh) & (c == yh // 2)

    barrier = pltpu.get_barrier_semaphore()

    def greet(dev):
        pl.semaphore_signal(barrier, inc=1, device_id=device(*dev), device_id_type=MESH)

    greet(sibling)
    for dx, fy in plane:
        greet(plane_dev(dx, fy))
    for dy in range(1, 4):
        greet((za, zb, (yh + dy) % 4, x, yl, c))
    greet((za, 1 - zb, yh, x, yl, c))
    for dza, fc in depth[:-1]:
        greet(far(dza, fc))
    met = 1 + 7 + 3 + 1 + 6
    for i in range(2):
        for h in range(2):

            @pl.when(jnp.logical_not(hid_target_is_me(i, h)))
            def _():
                greet(hid_target(i, h))

    for ys in range(4):

        @pl.when(jnp.logical_not(hid_source_is_me(ys)))
        def _():
            greet(hid_source(ys))

    own_hop = jnp.where((yl == zb) & (c == yh // 2), 1, 0)

    hid = hid_ref[...].astype(F32)
    gain = gain_ref[...].astype(F32)
    scaled = hid * gain
    for k in range(4):
        ht[k] = scaled[:, k * 128 : (k + 1) * 128].T.astype(BF16)

    def row_of(column):
        return jnp.broadcast_to(column, (128, 128)).T[0:8, :]

    def column_of(row):
        return jnp.broadcast_to(row[0:1, :], (128, 128)).T

    sums[0, 0] = row_of(jnp.sum(hid * hid, axis=1, keepdims=True))
    wall[c, za] = w_ref[pl.ds(pl.multiple_of(c * 128, 128), 128), :]

    pl.semaphore_wait(barrier, met + 8 - 2 * own_hop)

    def hid_copy(i, h):
        return remote(
            ht.at[2 * i + h],
            hall.at[zb, x, :, pl.ds(pl.multiple_of(yh * 128, 128), 128)],
            S_HID + 2 * i + h,
            hid_target(i, h),
            S_HID + yh,
        )

    def hid_arrival(ys):
        return remote(
            ht.at[0], hall.at[yl, x, :, ys * 128 : (ys + 1) * 128], S_HID + ys, sibling
        )

    for i in range(2):
        for h in range(2):

            @pl.when(jnp.logical_not(hid_target_is_me(i, h)))
            def _():
                hid_copy(i, h).start()

            @pl.when(hid_target_is_me(i, h))
            def _():
                own = pltpu.make_async_copy(
                    ht.at[2 * i + h],
                    hall.at[yl, x, :, pl.ds(pl.multiple_of(yh * 128, 128), 128)],
                    lsem,
                )
                own.start()
                own.wait()

    def sum_sibling(which, base):
        return remote(sums.at[which, 0], sums_in.at[which, 0], base, sibling)

    def sum_plane(which, base, n, dx, fy):
        return remote(
            sums.at[which, 1], sums_in.at[which, 1 + n], base + 1 + n, plane_dev(dx, fy)
        )

    sum_sibling(0, S_SQ).start()

    def w_copy(n, dza, fc):
        core = (c + fc) % 2
        return remote(
            w_ref.at[pl.ds(pl.multiple_of(core * 128, 128), 128), :],
            wall.at[c, za],
            S_W + n,
            far(dza, fc),
        )

    def w_arrival(n, dza, fc):
        return remote(
            w_ref.at[0:128, :], wall.at[(c + fc) % 2, (za + 4 - dza) % 4], S_W + n, sibling
        )

    for n, (dza, fc) in enumerate(depth):
        w_copy(n, dza, fc).start()

    rows = lax.broadcasted_iota(jnp.int32, (128, 128), 0)
    cols = lax.broadcasted_iota(jnp.int32, (128, 128), 1)
    causal = rows >= cols
    heads = ld_ref.shape[1]
    padded = jnp.concatenate([ld_ref[...], jnp.zeros((128, 128 - heads), F32)], axis=1)
    running = nn_dot(causal.astype(F32), padded, HIGHEST)
    running_t = running.T
    low = cols < MHEAD
    total = jnp.zeros((128, 128), F32)
    for p in range(heads // 2):
        xp = x_ref[:, p * 128 : (p + 1) * 128]
        zero = jnp.zeros_like(xp)
        both = jnp.concatenate([jnp.where(low, xp, zero), jnp.where(low, zero, xp)], axis=0)
        inner = nt_dot(dy_ref[:, p * 128 : (p + 1) * 128], both)
        for k in range(2):
            h = 2 * p + k
            gap = running[:, h : h + 1] - running_t[h : h + 1, :]
            decay = jnp.exp(jnp.where(causal, gap, -1e30))
            total = total + inner[:, k * 128 : (k + 1) * 128] * decay
    gram[0] = total
    gram_copy = remote(gram.at[0], gram.at[1], S_GRAM, sibling)
    gram_copy.start()

    sum_sibling(0, S_SQ).wait_recv()
    sums[0, 1] = sums[0, 0] + sums_in[0, 0]
    for n, (dx, fy) in enumerate(plane):
        sum_plane(0, S_SQ, n, dx, fy).start()

    gram_copy.wait_recv()
    total = gram[0] + gram[1]
    bc = bc_ref[...].astype(F32)
    grad_b = nn_dot(total.T, bc[:, 128:], HIGHEST)
    grad_c = nn_dot(total, bc[:, :128], HIGHEST)

    for n, (dx, fy) in enumerate(plane):
        sum_plane(0, S_SQ, n, dx, fy).wait_recv()
    square = sums[0, 1]
    for n in range(7):
        square = square + sums_in[0, 1 + n]
    mean_square = column_of(square) * (1.0 / 8192.0) + EPSILON
    inv_root = lax.rsqrt(mean_square)
    dall[c, zb, yh] = jnp.concatenate([grad_b * inv_root, grad_c * inv_root], axis=1).astype(BF16)

    def d_y(dy):
        block = dall.at[c, zb, yh]
        return remote(block, block, S_DY + dy, (za, zb, (yh + dy) % 4, x, yl, c))

    def d_z(dy):
        block = dall.at[c, zb, (yh + 4 - dy) % 4]
        return remote(block, block, S_DZ + dy, (za, 1 - zb, yh, x, yl, c))

    def d_c(k, dy):
        block = dall.at[c, (zb + k) % 2, (yh + 4 - dy) % 4]
        return remote(block, block, S_DC + 4 * k + dy, sibling)

    for dy in (2, 1, 3):
        d_y(dy).start()
    d_z(0).start()
    d_c(0, 0).start()

    def h_copy(n, dx, fy):
        block = hall.at[yl, x]
        return remote(block, block, S_HAG + n, plane_dev(dx, fy))

    def h_arrival(n, dx, fy):
        sx, sy = plane_src(dx, fy)
        return remote(hall.at[sy, sx], hall.at[sy, sx], S_HAG + n, sibling)

    for ys in range(4):

        @pl.when(jnp.logical_not(hid_source_is_me(ys)))
        def _():
            hid_arrival(ys).wait_recv()

    for n, (dx, fy) in enumerate(plane):
        h_copy(n, dx, fy).start()

    for dy in (1, 3, 2):
        d_y(dy).wait_recv()
        d_z(dy).start()
        d_c(0, dy).start()

    for n, (dza, fc) in enumerate(depth):
        w_arrival(n, dza, fc).wait_recv()

    def p_copy(n, dx, fy):
        tx, ty = (x + dx) % 4, (yl + fy) % 2
        return remote(psend.at[ty, tx], precv.at[yl, x], S_P + n, plane_dev(dx, fy))

    def p_arrival(n, dx, fy):
        sx, sy = plane_src(dx, fy)
        return remote(psend.at[sy, sx], precv.at[sy, sx], S_P + n, sibling)

    def terms(k):
        side = (zb + k) % 2
        for ys in range(4):
            out = nt_dot(dall[0, side, ys], wall[0].reshape(512, 256))
            out = out + nt_dot(dall[1, side, ys], wall[1].reshape(512, 256))
            for tx in range(4):
                psend[side, tx, ys * 128 : (ys + 1) * 128, :] = out[
                    :, tx * 128 : (tx + 1) * 128
                ].astype(BF16)

        @pl.when(side == yl)
        def _():
            for n, (dx, fy) in enumerate(plane):
                if fy == 0:
                    p_copy(n, dx, fy).start()

        @pl.when(side != yl)
        def _():
            for n, (dx, fy) in enumerate(plane):
                if fy == 1:
                    p_copy(n, dx, fy).start()

    for dy in (0, 1, 3, 2):
        d_c(0, dy).wait_recv()
    terms(0)
    for dy in (0, 1, 3, 2):
        d_z(dy).wait_recv()
        d_c(1, dy).start()
    for dy in (0, 1, 3, 2):
        d_c(1, dy).wait_recv()
    terms(1)

    def g_copy(n, dza, fc):
        return remote(
            gsend.at[(za + dza) % 4, (c + fc) % 2], grecv.at[za, c], S_G + n, far(dza, fc)
        )

    def g_arrival(n, dza, fc):
        return remote(
            gsend.at[0, 0], grecv.at[(za + 4 - dza) % 4, (c + fc) % 2], S_G + n, sibling
        )

    for n, (dx, fy) in enumerate(plane):
        h_arrival(n, dx, fy).wait_recv()
    for j in range(2):
        out = nn_dot(hall[0].reshape(512, 512), dall[j, 0].reshape(512, 256))
        out = out + nn_dot(hall[1].reshape(512, 512), dall[j, 1].reshape(512, 256))
        out = (out * (1.0 / 64.0)).astype(BF16)
        for k in range(4):
            gsend[k, j] = out[k * 128 : (k + 1) * 128, :]
    for n, (dza, fc) in enumerate(depth):
        g_copy(n, dza, fc).start()

    for n, (dx, fy) in enumerate(plane):
        p_arrival(n, dx, fy).wait_recv()
    acc = psend[yl, x].astype(F32)
    for n, (dx, fy) in enumerate(plane):
        sx, sy = plane_src(dx, fy)
        acc = acc + precv[sy, sx].astype(F32)
    rsum[...] = acc.astype(BF16).reshape(4, 128, 128)

    def q_copy(ys):
        return remote(
            rsum.at[ys], qrecv.at[yh % 2, c], S_Q + ys, hid_source(ys), S_Q + 2 * (yh % 2) + c
        )

    for ys in range(4):

        @pl.when(jnp.logical_not(hid_source_is_me(ys)))
        def _():
            q_copy(ys).start()

        @pl.when(hid_source_is_me(ys))
        def _():
            own = pltpu.make_async_copy(rsum.at[ys], qrecv.at[yh % 2, c], lsem)
            own.start()
            own.wait()

    for n, (dza, fc) in enumerate(depth):
        g_arrival(n, dza, fc).wait_recv()
    grecv[za, c] = gsend[za, c]
    for h in range(2):
        acc = grecv[0, h].astype(F32)
        for k in range(1, 4):
            acc = acc + grecv[k, h].astype(F32)
        wgrad_ref[h * 128 : (h + 1) * 128, :] = acc.astype(BF16)

    for i in range(2):
        for h in range(2):

            @pl.when(jnp.logical_not(hid_target_is_me(i, h)))
            def _():
                remote(
                    rsum.at[0], qrecv.at[i, h], S_Q + 2 * i + h, sibling
                ).wait_recv()

    grad = jnp.concatenate([qrecv[0, 0], qrecv[0, 1], qrecv[1, 0], qrecv[1, 1]], axis=1)
    grad = grad.astype(F32) * gain
    sums[1, 0] = row_of(jnp.sum(grad * hid, axis=1, keepdims=True))
    sum_sibling(1, S_MEAN).start()
    sum_sibling(1, S_MEAN).wait_recv()
    sums[1, 1] = sums[1, 0] + sums_in[1, 0]
    for n, (dx, fy) in enumerate(plane):
        sum_plane(1, S_MEAN, n, dx, fy).start()
    for n, (dx, fy) in enumerate(plane):
        sum_plane(1, S_MEAN, n, dx, fy).wait_recv()
    dot = sums[1, 1]
    for n in range(7):
        dot = dot + sums_in[1, 1 + n]
    factor = column_of(dot) * (1.0 / 8192.0) / mean_square
    for k in range(4):
        part = slice(k * 128, (k + 1) * 128)
        igrad_ref[:, part] = (grad[:, part] - hid[:, part] * factor).astype(BF16)

    for i in range(2):
        for h in range(2):

            @pl.when(jnp.logical_not(hid_target_is_me(i, h)))
            def _():
                hid_copy(i, h).wait_send()

    for ys in range(4):

        @pl.when(jnp.logical_not(hid_source_is_me(ys)))
        def _():
            q_copy(ys).wait_send()

    for which, base in ((0, S_SQ), (1, S_MEAN)):
        sum_sibling(which, base).wait_send()
        for n, (dx, fy) in enumerate(plane):
            sum_plane(which, base, n, dx, fy).wait_send()
    gram_copy.wait_send()
    for n, (dza, fc) in enumerate(depth):
        w_copy(n, dza, fc).wait_send()
        g_copy(n, dza, fc).wait_send()
    for n, (dx, fy) in enumerate(plane):
        h_copy(n, dx, fy).wait_send()
        p_copy(n, dx, fy).wait_send()
    for dy in range(4):
        if dy:
            d_y(dy).wait_send()
        d_z(dy).wait_send()
        d_c(0, dy).wait_send()
        d_c(1, dy).wait_send()


def shards(hidden, gain, proj_weight, b_c, ssm_x, dy, log_decay):
    vmem = pl.BlockSpec(memory_space=pltpu.VMEM)
    return pl.pallas_call(
        kernel,
        out_shape=(
            jax.ShapeDtypeStruct(hidden.shape, BF16),
            jax.ShapeDtypeStruct(proj_weight.shape, BF16),
        ),
        in_specs=[vmem] * 7,
        out_specs=(vmem, vmem),
        scratch_shapes=[
            pltpu.VMEM((4, 128, 128), BF16),
            pltpu.VMEM((2, 4, 128, 512), BF16),
            pltpu.VMEM((2, 4, 128, 256), BF16),
            pltpu.VMEM((2, 2, 8, 128), F32),
            pltpu.VMEM((2, 8, 8, 128), F32),
            pltpu.VMEM((2, 128, 128), F32),
            pltpu.VMEM((2, 2, 4, 128, 256), BF16),
            pltpu.VMEM((2, 4, 512, 128), BF16),
            pltpu.VMEM((2, 4, 512, 128), BF16),
            pltpu.VMEM((4, 128, 128), BF16),
            pltpu.VMEM((2, 2, 128, 128), BF16),
            pltpu.VMEM((4, 2, 128, 256), BF16),
            pltpu.VMEM((4, 2, 128, 256), BF16),
            pltpu.SemaphoreType.DMA((N_SLOTS,)),
            pltpu.SemaphoreType.DMA((N_SLOTS,)),
            pltpu.SemaphoreType.DMA,
        ],
        compiler_params=pltpu.CompilerParams(
            collective_id=0, has_side_effects=True, vmem_limit_bytes=40 * 1024 * 1024
        ),
        name="projection_backward",
    )(hidden, gain.reshape(1, -1), proj_weight, b_c, ssm_x, dy, log_decay)


def solution(mesh):
    return jax.shard_map(
        shards,
        mesh=mesh,
        in_specs=(
            P("dp", "tensor"),
            P("tensor"),
            P("dp", "tensor"),
            P("dp", "tensor"),
            P("dp", "tensor"),
            P("dp", "tensor"),
            P("dp", "tensor"),
        ),
        out_specs=(P("dp", "tensor"), P("dp", "tensor")),
        check_vma=False,
    )
```

```python
import jax
import jax.numpy as jnp
from jax import lax
from jax.experimental import pallas as pl
from jax.experimental.pallas import tpu as pltpu
from jax.sharding import PartitionSpec as P

MHEAD = 64
EPSILON = 1e-05
MESH = pl.DeviceIdType.MESH
F32 = jnp.float32
BF16 = jnp.bfloat16
HIGHEST = lax.Precision.HIGHEST


def device(za, zb, yh, x, yl, c):
    return {"dp": (za * 2 + zb) * 4 + yh, "tensor": x * 4 + yl * 2 + c}


def nt_dot(a, b, precision=None):
    return lax.dot_general(
        a, b, (((1,), (1,)), ((), ())), preferred_element_type=F32, precision=precision
    )


def nn_dot(a, b, precision=None):
    return lax.dot_general(
        a, b, (((1,), (0,)), ((), ())), preferred_element_type=F32, precision=precision
    )


class Slots:
    def __init__(self):
        self.count = 0

    def take(self, n):
        first = self.count
        self.count += n
        return first


SLOTS = Slots()
S_HID = SLOTS.take(4)
S_HAG = SLOTS.take(14)
S_W = SLOTS.take(7)
S_SQ = SLOTS.take(8)
S_INV = SLOTS.take(8)
S_GRAM = SLOTS.take(1)
S_DY = SLOTS.take(4)
S_DZ = SLOTS.take(4)
S_DC = SLOTS.take(8)
S_P = SLOTS.take(14)
S_Q = SLOTS.take(4)
S_G = SLOTS.take(7)
S_DOT = SLOTS.take(8)
S_MEAN = SLOTS.take(15)
N_SLOTS = SLOTS.count


def kernel(
    hid_hbm,
    gain_hbm,
    w_hbm,
    bc_hbm,
    x_hbm,
    dy_hbm,
    ld_hbm,
    igrad_hbm,
    wgrad_hbm,
    igrad_ref,
    wgrad_ref,
    hid_ref,
    gain_ref,
    w_ref,
    bc_ref,
    x_ref,
    dy_ref,
    ld_ref,
    ht,
    hall,
    hscaled,
    wall,
    sums,
    sums_in,
    inv,
    dots,
    dots_in,
    gram,
    dall,
    psend,
    precv,
    rsum,
    qrecv,
    gsend,
    grecv,
    grelay,
    ssem,
    rsem,
    lsem,
    isem,
):
    loads = [
        pltpu.make_async_copy(src, dst, isem.at[n])
        for n, (src, dst) in enumerate(
            (
                (ld_hbm, ld_ref),
                (x_hbm, x_ref),
                (dy_hbm, dy_ref),
                (hid_hbm, hid_ref),
                (gain_hbm, gain_ref),
                (w_hbm, w_ref),
                (bc_hbm, bc_ref),
            )
        )
    ]
    for load in loads:
        load.start()

    dp = lax.axis_index("dp")
    ten = lax.axis_index("tensor")
    z, yh = dp // 4, dp % 4
    za, zb = z // 2, z % 2
    x, yl, c = ten // 4, (ten // 2) % 2, ten % 2

    def remote(src, dst, slot, dev, rslot=None):
        rslot = slot if rslot is None else rslot
        return pltpu.make_async_remote_copy(
            src_ref=src,
            dst_ref=dst,
            send_sem=ssem.at[slot],
            recv_sem=rsem.at[rslot],
            device_id=device(*dev),
            device_id_type=MESH,
        )

    sibling = (za, zb, yh, x, yl, 1 - c)
    plane = [(1, 0), (3, 0), (2, 0), (0, 1), (1, 1), (3, 1), (2, 1)]
    column = [(0, 1), (0, 3), (0, 2), (1, 0), (1, 1), (1, 3), (1, 2)]
    depth = [(dza, fc) for dza in (1, 3) for fc in range(2)] + [(0, 1)]
    tensor = [(0, 0, 1)] + [(dx, fy, fc) for fc in range(2) for dx, fy in plane]

    def plane_dev(dx, fy):
        return (za, zb, yh, (x + dx) % 4, (yl + fy) % 2, c)

    def plane_src(dx, fy):
        return (x + 4 - dx) % 4, (yl + fy) % 2

    def tensor_dev(dx, fy, fc):
        return (za, zb, yh, (x + dx) % 4, (yl + fy) % 2, (c + fc) % 2)

    def column_dev(k, dy):
        return (za, (zb + k) % 2, (yh + dy) % 4, x, yl, c)

    def far(dza, fc):
        return ((za + dza) % 4, zb, yh, x, yl, (c + fc) % 2)

    def seq(side, y):
        return (y % 2, side, y // 2)

    def hid_target(i, h):
        return (za, yl, 2 * c + i, x, yh % 2, h)

    def hid_target_is_me(i, h):
        return (yl == zb) & (yh == 2 * c + i) & (yl == yh % 2) & (c == h)

    def hid_source(side, u):
        return (za, side, yl + 2 * u, x, zb, yh // 2)

    def hid_source_is_me(side, u):
        return (side == zb) & (yl + 2 * u == yh) & (yl == zb) & (c == yh // 2)

    barrier = pltpu.get_barrier_semaphore()

    def greet(dev):
        pl.semaphore_signal(barrier, inc=1, device_id=device(*dev), device_id_type=MESH)

    for dx, fy, fc in tensor:
        greet(tensor_dev(dx, fy, fc))
    for k, dy in column:
        greet(column_dev(k, dy))
    for dza, fc in depth[:-1]:
        greet(far(dza, fc))
    met = 15 + 7 + 4
    for i in range(2):
        for h in range(2):

            @pl.when(jnp.logical_not(hid_target_is_me(i, h)))
            def _():
                greet(hid_target(i, h))

    for side in range(2):
        for u in range(2):

            @pl.when(jnp.logical_not(hid_source_is_me(side, u)))
            def _():
                greet(hid_source(side, u))

    own_hop = jnp.where((yl == zb) & (yl == yh % 2) & (c == yh // 2), 1, 0)

    for load in loads[:3]:
        load.wait()
    rows = lax.broadcasted_iota(jnp.int32, (128, 128), 0)
    cols = lax.broadcasted_iota(jnp.int32, (128, 128), 1)
    causal = rows >= cols
    heads = ld_ref.shape[0]
    padded = jnp.concatenate([ld_ref[...], jnp.zeros((128 - heads, 128), F32)], axis=0)
    running_t = nt_dot(padded, causal.astype(F32), HIGHEST)
    running = running_t.T
    low = cols < MHEAD
    total = jnp.zeros((128, 128), F32)
    for p in range(heads // 2):
        xp = x_ref[:, p * 128 : (p + 1) * 128]
        zero = jnp.zeros_like(xp)
        both = jnp.concatenate([jnp.where(low, xp, zero), jnp.where(low, zero, xp)], axis=0)
        inner = nt_dot(dy_ref[:, p * 128 : (p + 1) * 128], both)
        for k in range(2):
            h = 2 * p + k
            gap = running[:, h : h + 1] - running_t[h : h + 1, :]
            decay = jnp.exp(jnp.where(causal, gap, -1e30))
            total = total + inner[:, k * 128 : (k + 1) * 128] * decay
    gram[0] = total

    for load in loads[3:]:
        load.wait()
    hid = hid_ref[...].astype(F32)
    gain = gain_ref[...].astype(F32).reshape(1, -1)
    scaled = hid * gain
    for k in range(4):
        ht[k] = scaled[:, k * 128 : (k + 1) * 128].T.astype(BF16)

    def row_of(column):
        return jnp.broadcast_to(column, (128, 128)).T[0:8, :]

    def column_of(row):
        return jnp.broadcast_to(row[0:1, :], (128, 128)).T

    sums[0] = row_of(jnp.sum(hid * hid, axis=1, keepdims=True))
    wall[c, za] = w_ref[pl.ds(pl.multiple_of(c * 128, 128), 128), :]

    pl.semaphore_wait(barrier, met + 8 - 2 * own_hop)

    gram_copy = remote(gram.at[0], gram.at[1], S_GRAM, sibling)
    gram_copy.start()

    sq_sibling = remote(sums.at[0], sums_in.at[0, 0], S_SQ, sibling)
    sq_sibling.start()

    def sq_copy(n):
        return remote(sums.at[1], sums_in.at[0, 1 + n], S_SQ + 1 + n, plane_dev(*plane[n]))

    def mean_copy(n):
        return remote(sums.at[2], sums_in.at[1, n], S_MEAN + n, tensor_dev(*tensor[n]))

    def hid_copy(i, h):
        lane = (2 * zb + yh // 2) * 128
        return remote(
            ht.at[2 * i + h],
            hall.at[yh % 2, x, :, pl.ds(pl.multiple_of(lane, 128), 128)],
            S_HID + 2 * i + h,
            hid_target(i, h),
            S_HID + 2 * zb + yh // 2,
        )

    def hid_arrival(side, u):
        lane = (2 * side + u) * 128
        return remote(
            ht.at[0],
            hall.at[yl, x, :, pl.ds(pl.multiple_of(lane, 128), 128)],
            S_HID + 2 * side + u,
            sibling,
        )

    for i in range(2):
        for h in range(2):

            @pl.when(jnp.logical_not(hid_target_is_me(i, h)))
            def _():
                hid_copy(i, h).start()

            @pl.when(hid_target_is_me(i, h))
            def _():
                lane = (2 * zb + yh // 2) * 128
                own = pltpu.make_async_copy(
                    ht.at[2 * i + h],
                    hall.at[yl, x, :, pl.ds(pl.multiple_of(lane, 128), 128)],
                    lsem,
                )
                own.start()
                own.wait()

    def w_copy(n):
        dza, fc = depth[n]
        core = (c + fc) % 2
        return remote(
            w_ref.at[pl.ds(pl.multiple_of(core * 128, 128), 128), :],
            wall.at[c, za],
            S_W + n,
            far(dza, fc),
        )

    def w_arrival(n):
        dza, fc = depth[n]
        return remote(
            w_ref.at[0:128, :], wall.at[(c + fc) % 2, (za + 4 - dza) % 4], S_W + n, sibling
        )

    for n in range(5):
        w_copy(n).start()

    def w_on(j):
        block = wall.at[j, (za + (1, 3)[j] + 2) % 4]
        return remote(block, block, S_W + 5 + j, far((1, 3)[j], 0))

    def w_on_arrival(j):
        block = wall.at[j, (za + 2) % 4]
        return remote(block, block, S_W + 5 + j, sibling)

    sq_sibling.wait_recv()
    sums[1] = sums[0] + sums_in[0, 0]
    for n in range(7):
        sq_copy(n).start()

    gram_copy.wait_recv()
    total = gram[0] + gram[1]
    bc = bc_ref[...].astype(F32)
    grad_b = nn_dot(total.T, bc[:, 128:], HIGHEST)
    grad_c = nn_dot(total, bc[:, :128], HIGHEST)
    dall[(c,) + seq(zb, yh)] = jnp.concatenate([grad_b, grad_c], axis=1).astype(BF16)

    def d_y(dy):
        block = dall.at[(c,) + seq(zb, yh)]
        return remote(block, block, S_DY + dy, column_dev(0, dy))

    def d_y_arrival(dy):
        block = dall.at[(c,) + seq(zb, (yh + 4 - dy) % 4)]
        return remote(block, block, S_DY + dy, sibling)

    def d_z(dy):
        if dy == 2:
            block = dall.at[(c,) + seq(1 - zb, yh)]
            return remote(block, block, S_DZ + dy, column_dev(0, 2))
        block = dall.at[(c,) + seq(zb, (yh + 4 - dy) % 4)]
        return remote(block, block, S_DZ + dy, column_dev(1, 0))

    def d_z_arrival(dy):
        block = dall.at[(c,) + seq(1 - zb, (yh + 4 - dy) % 4)]
        return remote(block, block, S_DZ + dy, sibling)

    def d_c(k, dy):
        block = dall.at[(c,) + seq((zb + k) % 2, (yh + 4 - dy) % 4)]
        return remote(block, block, S_DC + 4 * k + dy, sibling)

    def d_c_arrival(k, dy):
        block = dall.at[(1 - c,) + seq((zb + k) % 2, (yh + 4 - dy) % 4)]
        return remote(block, block, S_DC + 4 * k + dy, sibling)

    for dy in (1, 3):
        d_y(dy).start()
    d_z(0).start()
    d_c(0, 0).start()

    square = sums[1]
    for n in range(7):
        sq_copy(n).wait_recv()
        square = square + sums_in[0, 1 + n]
    mean_square = square * (1.0 / 8192.0) + EPSILON
    inv_root = lax.rsqrt(mean_square)
    inv[seq(zb, yh)] = inv_root

    def inv_copy(n):
        block = inv.at[seq(zb, yh)]
        return remote(block, block, S_INV + n, column_dev(*column[n]))

    def inv_arrival(n):
        k, dy = column[n]
        block = inv.at[seq((zb + k) % 2, (yh + 4 - dy) % 4)]
        return remote(block, block, S_INV + n, sibling)

    for n in range(7):
        inv_copy(n).start()

    def h_block(k, sy, sx):
        lane = ((zb + k) % 2) * 256
        return hall.at[sy, sx, :, pl.ds(pl.multiple_of(lane, 128), 256)]

    def h_copy(k, n):
        dx, fy = plane[n]
        block = h_block(k, (yl + fy) % 2 if dx else yl, x)
        dev = (za, zb, yh, (x + dx) % 4, yl if dx else 1 - yl, c)
        return remote(block, block, S_HAG + 7 * k + n, dev)

    def h_arrival(k, n):
        sx, sy = plane_src(*plane[n])
        block = h_block(k, sy, sx)
        return remote(block, block, S_HAG + 7 * k + n, sibling)

    def hid_on(k):
        side = (zb + k) % 2
        for u in range(2):

            @pl.when(jnp.logical_not(hid_source_is_me(side, u)))
            def _():
                hid_arrival(side, u).wait_recv()

        for n in (3, 0, 1, 2):
            h_copy(k, n).start()

    def hid_across(k):
        h_arrival(k, 3).wait_recv()
        for n in range(4, 7):
            h_copy(k, n).start()

    hid_on(0)
    hid_on(1)
    d_y(2).start()

    def d_on(dy):
        d_y_arrival(dy).wait_recv()
        if dy != 2:
            d_z(dy).start()
        d_c(0, dy).start()

    d_on(1)
    d_on(3)
    hid_across(0)
    d_z_arrival(0).wait_recv()
    d_z(2).start()
    d_c(1, 0).start()
    for n in range(4):
        w_arrival(n).wait_recv()
    for j in range(2):
        w_on(j).start()
    hid_across(1)
    d_on(2)

    for dy in (0, 1, 3, 2):
        d_c_arrival(0, dy).wait_recv()

    def p_copy(k, n):
        dx, fy = plane[n]
        side = (zb + k) % 2
        return remote(
            psend.at[side, (yl + fy) % 2, (x + dx) % 4],
            precv.at[side, yl, x],
            S_P + 7 * k + n,
            plane_dev(dx, fy),
        )

    def p_arrival(k, n):
        sx, sy = plane_src(*plane[n])
        block = precv.at[(zb + k) % 2, sy, sx]
        return remote(block, block, S_P + 7 * k + n, sibling)

    def terms(k, dza):
        side, tx = (zb + k) % 2, (za + dza) % 4
        for py in range(2):
            out = nt_dot(dall[0, py, side].reshape(256, 256), wall[0, tx])
            out = out + nt_dot(dall[1, py, side].reshape(256, 256), wall[1, tx])
            psend[side, py, tx] = out.astype(BF16)

    def p_start(k, dza):
        for n, (dx, fy) in enumerate(plane):

            @pl.when((x + dx) % 4 == (za + dza) % 4)
            def _():
                p_copy(k, n).start()

    w_arrival(4).wait_recv()
    terms(0, 0)
    p_start(0, 0)
    terms(0, 1)
    p_start(0, 1)
    terms(0, 3)
    p_start(0, 3)
    for j in range(2):
        w_on_arrival(j).wait_recv()
    terms(0, 2)
    p_start(0, 2)
    for dy in (1, 3, 2):
        d_z_arrival(dy).wait_recv()
        d_c(1, dy).start()
    for dy in (0, 1, 3, 2):
        d_c_arrival(1, dy).wait_recv()
    for dza in range(4):
        terms(1, dza)

    def g_copy(d, j):
        dza = (1, 3)[d]
        dev = ((za + dza) % 4, zb, yh, x, yl, j)
        return remote(
            gsend.at[(za + dza) % 4, j], grecv.at[za, c], S_G + 2 * d + j, dev, S_G + 2 * d + c
        )

    def g_arrival(d, h):
        block = grecv.at[(za + (3, 1)[d]) % 4, h]
        return remote(block, block, S_G + 2 * d + h, sibling)

    def g_sibling():
        return remote(gsend.at[za, 1 - c], grecv.at[za, c], S_G + 4, sibling)

    def g_relay(j):
        return remote(
            gsend.at[(za + 2) % 4, j], grelay.at[j], S_G + 5 + j, far((1, 3)[j], 0)
        )

    for n in range(7):
        inv_arrival(n).wait_recv()
    inv_rows = [
        jnp.concatenate([inv[sy, side, u][0:1, :] for side in range(2) for u in range(2)], axis=1)
        for sy in range(2)
    ]
    inv_rows = [inv_rows[sy] * (1.0 / 64.0) for sy in range(2)]
    own_inv = jnp.where(yl == 0, inv_rows[0], inv_rows[1])
    other_inv = jnp.where(yl == 0, inv_rows[1], inv_rows[0])

    def scale(dx, fy):
        sx, sy = plane_src(dx, fy)
        row = other_inv if fy else own_inv
        hscaled[sy, sx] = (hall[sy, sx].astype(F32) * row).astype(BF16)

    scale(0, 0)
    scale(0, 1)
    for n in (0, 1, 2, 4, 5, 6):
        h_arrival(0, n).wait_recv()
        h_arrival(1, n).wait_recv()
        scale(*plane[n])
    eye = (rows == cols).astype(F32)
    for py in range(2):
        for side in range(2):
            for u in range(2):
                part = slice(u * 128, (u + 1) * 128)
                lane = (2 * side + u) * 128
                prod = jnp.zeros((128, 128), F32)
                for f in range(4):
                    prod = prod + nn_dot(
                        psend[side, py, f, part, :], hall[py, f, :, lane : lane + 128]
                    )
                row = jnp.sum(prod * eye, axis=0, keepdims=True)
                dots[py, side, u] = jnp.broadcast_to(row, (8, 128))

    def dot_copy(n):
        k, dy = column[n]
        block = dots.at[seq((zb + k) % 2, (yh + dy) % 4)]
        return remote(block, dots_in.at[n], S_DOT + n, column_dev(k, dy))

    for n in range(7):
        dot_copy(n).start()
    for n in range(7):
        p_copy(1, n).start()

    for j in range(2):
        out = nn_dot(hscaled[0].reshape(512, 512), dall[j, 0].reshape(512, 256))
        out = out + nn_dot(hscaled[1].reshape(512, 512), dall[j, 1].reshape(512, 256))
        out = out.astype(BF16)
        for k in range(4):
            gsend[k, j] = out[k * 128 : (k + 1) * 128, :]
    for j in range(2):
        g_relay(j).start()
    g_copy(0, 1).start()
    g_copy(1, 0).start()
    g_sibling().start()

    def q_copy(k, u):
        side = (zb + k) % 2
        return remote(
            rsum.at[side, u],
            qrecv.at[yh % 2, c],
            S_Q + 2 * k + u,
            hid_source(side, u),
            S_Q + 2 * (yh % 2) + c,
        )

    def owners(k):
        side = (zb + k) % 2
        for n in range(7):
            p_arrival(k, n).wait_recv()
        acc = psend[side, yl, x].astype(F32)
        for n in range(7):
            sx, sy = plane_src(*plane[n])
            acc = acc + precv[side, sy, sx].astype(F32)
        rsum[side] = acc.astype(BF16).reshape(2, 128, 128)
        for u in range(2):

            @pl.when(jnp.logical_not(hid_source_is_me(side, u)))
            def _():
                q_copy(k, u).start()

            @pl.when(hid_source_is_me(side, u))
            def _():
                own = pltpu.make_async_copy(rsum.at[side, u], qrecv.at[yh % 2, c], lsem)
                own.start()
                own.wait()

    owners(0)
    for j in range(2):
        g_relay(j).wait_recv()
        to = (za + (1, 3)[j]) % 4
        gsend[to, j] = (gsend[to, j].astype(F32) + grelay[j].astype(F32)).astype(BF16)
        g_copy(j, j).start()

    for n in range(7):
        dot_copy(n).wait_recv()
    value = dots[seq(zb, yh)]
    for n in range(7):
        value = value + dots_in[n]
    sums[2] = value
    for n in range(15):
        mean_copy(n).start()
    owners(1)

    g_sibling().wait_recv()
    for h in range(2):
        for d in range(2):
            g_arrival(d, h).wait_recv()
    grecv[za, c] = gsend[za, c]
    for h in range(2):
        acc = grecv[za, h].astype(F32)
        for d in range(2):
            acc = acc + grecv[(za + (3, 1)[d]) % 4, h].astype(F32)
        wgrad_ref[h * 128 : (h + 1) * 128, :] = acc.astype(BF16)

    wgrad_out = pltpu.make_async_copy(wgrad_ref, wgrad_hbm, isem.at[7])
    wgrad_out.start()
    dot = sums[2]
    for n in range(15):
        mean_copy(n).wait_recv()
        dot = dot + sums_in[1, n]
    factor = column_of(dot * (1.0 / 8192.0) / mean_square)
    inv_column = column_of(inv_root)
    for i in range(2):
        for h in range(2):

            @pl.when(jnp.logical_not(hid_target_is_me(i, h)))
            def _():
                remote(rsum.at[0, 0], qrecv.at[i, h], S_Q + 2 * i + h, sibling).wait_recv()

    for i in range(2):
        for h in range(2):
            k = 2 * i + h
            part = slice(k * 128, (k + 1) * 128)
            grad = qrecv[i, h].astype(F32) * gain[:, part]
            igrad_ref[:, part] = ((grad - hid[:, part] * factor) * inv_column).astype(BF16)

    igrad_out = pltpu.make_async_copy(igrad_ref, igrad_hbm, isem.at[8])
    igrad_out.start()

    for i in range(2):
        for h in range(2):

            @pl.when(jnp.logical_not(hid_target_is_me(i, h)))
            def _():
                hid_copy(i, h).wait_send()

    for k in range(2):
        for u in range(2):

            @pl.when(jnp.logical_not(hid_source_is_me((zb + k) % 2, u)))
            def _():
                q_copy(k, u).wait_send()

    sq_sibling.wait_send()
    for n in range(7):
        sq_copy(n).wait_send()
    for n in range(15):
        mean_copy(n).wait_send()
    gram_copy.wait_send()
    for n in range(5):
        w_copy(n).wait_send()
    g_sibling().wait_send()
    for j in range(2):
        w_on(j).wait_send()
        g_relay(j).wait_send()
        for d in range(2):
            g_copy(d, j).wait_send()
    for n in range(7):
        h_copy(0, n).wait_send()
        h_copy(1, n).wait_send()
        p_copy(0, n).wait_send()
        p_copy(1, n).wait_send()
        inv_copy(n).wait_send()
        dot_copy(n).wait_send()
    for dy in range(4):
        if dy:
            d_y(dy).wait_send()
        d_z(dy).wait_send()
        d_c(0, dy).wait_send()
        d_c(1, dy).wait_send()
    wgrad_out.wait()
    igrad_out.wait()


def hand_over(igrad_ref, wgrad_ref, igrad_out, wgrad_out, igrad, wgrad, sem):
    ins = [
        pltpu.make_async_copy(igrad_ref, igrad, sem.at[0]),
        pltpu.make_async_copy(wgrad_ref, wgrad, sem.at[1]),
    ]
    outs = [
        pltpu.make_async_copy(igrad, igrad_out, sem.at[2]),
        pltpu.make_async_copy(wgrad, wgrad_out, sem.at[3]),
    ]
    for copy in ins:
        copy.start()
    for first, second in zip(ins, outs):
        first.wait()
        second.start()
    for copy in outs:
        copy.wait()


def shards(hidden, gain, proj_weight, b_c, ssm_x, dy, log_decay):
    hbm = pl.BlockSpec(memory_space=pl.ANY)
    grads = pl.pallas_call(
        kernel,
        out_shape=(
            jax.ShapeDtypeStruct(hidden.shape, BF16),
            jax.ShapeDtypeStruct(proj_weight.shape, BF16),
        ),
        in_specs=[hbm] * 7,
        out_specs=(hbm, hbm),
        scratch_shapes=[
            pltpu.VMEM(hidden.shape, BF16),
            pltpu.VMEM(proj_weight.shape, BF16),
            pltpu.VMEM(hidden.shape, BF16),
            pltpu.VMEM(gain.shape, BF16),
            pltpu.VMEM(proj_weight.shape, BF16),
            pltpu.VMEM(b_c.shape, BF16),
            pltpu.VMEM(ssm_x.shape, BF16),
            pltpu.VMEM(dy.shape, BF16),
            pltpu.VMEM(log_decay.shape[::-1], F32),
            pltpu.VMEM((4, 128, 128), BF16),
            pltpu.VMEM((2, 4, 128, 512), BF16),
            pltpu.VMEM((2, 4, 128, 512), BF16),
            pltpu.VMEM((2, 4, 128, 256), BF16),
            pltpu.VMEM((3, 8, 128), F32),
            pltpu.VMEM((2, 15, 8, 128), F32),
            pltpu.VMEM((2, 2, 2, 8, 128), F32),
            pltpu.VMEM((2, 2, 2, 8, 128), F32),
            pltpu.VMEM((7, 8, 128), F32),
            pltpu.VMEM((2, 128, 128), F32),
            pltpu.VMEM((2, 2, 2, 2, 128, 256), BF16),
            pltpu.VMEM((2, 2, 4, 256, 128), BF16),
            pltpu.VMEM((2, 2, 4, 256, 128), BF16),
            pltpu.VMEM((2, 2, 128, 128), BF16),
            pltpu.VMEM((2, 2, 128, 128), BF16),
            pltpu.VMEM((4, 2, 128, 256), BF16),
            pltpu.VMEM((4, 2, 128, 256), BF16),
            pltpu.VMEM((2, 128, 256), BF16),
            pltpu.SemaphoreType.DMA((N_SLOTS,)),
            pltpu.SemaphoreType.DMA((N_SLOTS,)),
            pltpu.SemaphoreType.DMA,
            pltpu.SemaphoreType.DMA((9,)),
        ],
        compiler_params=pltpu.CompilerParams(
            collective_id=0, has_side_effects=True, vmem_limit_bytes=63 * 1024 * 1024
        ),
        name="projection_backward",
    )(hidden, gain, proj_weight, b_c, ssm_x, dy, log_decay.T)
    return pl.pallas_call(
        hand_over,
        out_shape=tuple(jax.ShapeDtypeStruct(grad.shape, grad.dtype) for grad in grads),
        in_specs=[hbm] * 2,
        out_specs=(hbm, hbm),
        scratch_shapes=[
            pltpu.VMEM(hidden.shape, BF16),
            pltpu.VMEM(proj_weight.shape, BF16),
            pltpu.SemaphoreType.DMA((4,)),
        ],
        compiler_params=pltpu.CompilerParams(vmem_limit_bytes=63 * 1024 * 1024),
        name="hand_over",
    )(*grads)


def solution(mesh):
    return jax.shard_map(
        shards,
        mesh=mesh,
        in_specs=(
            P("dp", "tensor"),
            P("tensor"),
            P("dp", "tensor"),
            P("dp", "tensor"),
            P("dp", "tensor"),
            P("dp", "tensor"),
            P("dp", "tensor"),
        ),
        out_specs=(P("dp", "tensor"), P("dp", "tensor")),
        check_vma=False,
    )
```

```python
import jax
import jax.numpy as jnp
from jax import lax
from jax.experimental import pallas as pl
from jax.experimental.pallas import tpu as pltpu
from jax.sharding import PartitionSpec as P

MHEAD = 64
EPSILON = 1e-05
MESH = pl.DeviceIdType.MESH
F32 = jnp.float32
BF16 = jnp.bfloat16
HIGHEST = lax.Precision.HIGHEST


def device(za, zb, yh, x, yl, c):
    return {"dp": (za * 2 + zb) * 4 + yh, "tensor": x * 4 + yl * 2 + c}


def nt_dot(a, b, precision=None):
    return lax.dot_general(
        a, b, (((1,), (1,)), ((), ())), preferred_element_type=F32, precision=precision
    )


def nn_dot(a, b, precision=None):
    return lax.dot_general(
        a, b, (((1,), (0,)), ((), ())), preferred_element_type=F32, precision=precision
    )


class Slots:
    def __init__(self):
        self.count = 0

    def take(self, n):
        first = self.count
        self.count += n
        return first


SLOTS = Slots()
S_HID = SLOTS.take(4)
S_HAG = SLOTS.take(14)
S_W = SLOTS.take(7)
S_SQ = SLOTS.take(8)
S_INV = SLOTS.take(8)
S_GRAM = SLOTS.take(1)
S_DY = SLOTS.take(4)
S_DZ = SLOTS.take(4)
S_DC = SLOTS.take(8)
S_P = SLOTS.take(14)
S_Q = SLOTS.take(4)
S_G = SLOTS.take(7)
S_DOT = SLOTS.take(8)
S_MEAN = SLOTS.take(15)
N_SLOTS = SLOTS.count


def kernel(
    hid_hbm,
    gain_hbm,
    w_hbm,
    bc_hbm,
    x_hbm,
    dy_hbm,
    ld_hbm,
    igrad_hbm,
    wgrad_hbm,
    igrad_ref,
    wgrad_ref,
    hid_ref,
    gain_ref,
    w_ref,
    bc_ref,
    x_ref,
    dy_ref,
    ld_ref,
    ht,
    hall,
    hscaled,
    wall,
    sums,
    sums_in,
    inv,
    dots,
    dots_in,
    gram,
    dall,
    psend,
    precv,
    rsum,
    qrecv,
    gsend,
    grecv,
    grelay,
    prelay,
    ssem,
    rsem,
    lsem,
    isem,
):
    loads = [
        pltpu.make_async_copy(src, dst, isem.at[n])
        for n, (src, dst) in enumerate(
            (
                (ld_hbm, ld_ref),
                (x_hbm, x_ref),
                (dy_hbm, dy_ref),
                (hid_hbm, hid_ref),
                (gain_hbm, gain_ref),
                (w_hbm, w_ref),
                (bc_hbm, bc_ref),
            )
        )
    ]
    for load in loads:
        load.start()

    dp = lax.axis_index("dp")
    ten = lax.axis_index("tensor")
    z, yh = dp // 4, dp % 4
    za, zb = z // 2, z % 2
    x, yl, c = ten // 4, (ten // 2) % 2, ten % 2

    def remote(src, dst, slot, dev, rslot=None):
        rslot = slot if rslot is None else rslot
        return pltpu.make_async_remote_copy(
            src_ref=src,
            dst_ref=dst,
            send_sem=ssem.at[slot],
            recv_sem=rsem.at[rslot],
            device_id=device(*dev),
            device_id_type=MESH,
        )

    sibling = (za, zb, yh, x, yl, 1 - c)
    plane = [(1, 0), (3, 0), (2, 0), (0, 1), (1, 1), (3, 1), (2, 1)]
    column = [(0, 1), (0, 3), (0, 2), (1, 0), (1, 1), (1, 3), (1, 2)]
    depth = [(dza, fc) for dza in (1, 3) for fc in range(2)] + [(0, 1)]
    tensor = [(0, 0, 1)] + [(dx, fy, fc) for fc in range(2) for dx, fy in plane]

    def plane_dev(dx, fy):
        return (za, zb, yh, (x + dx) % 4, (yl + fy) % 2, c)

    def plane_src(dx, fy):
        return (x + 4 - dx) % 4, (yl + fy) % 2

    def tensor_dev(dx, fy, fc):
        return (za, zb, yh, (x + dx) % 4, (yl + fy) % 2, (c + fc) % 2)

    def column_dev(k, dy):
        return (za, (zb + k) % 2, (yh + dy) % 4, x, yl, c)

    def far(dza, fc):
        return ((za + dza) % 4, zb, yh, x, yl, (c + fc) % 2)

    def seq(side, y):
        return (y % 2, side, y // 2)

    def hid_target(i, h):
        return (za, yl, 2 * c + i, x, yh % 2, h)

    def hid_target_is_me(i, h):
        return (yl == zb) & (yh == 2 * c + i) & (yl == yh % 2) & (c == h)

    def hid_source(side, u):
        return (za, side, yl + 2 * u, x, zb, yh // 2)

    def hid_source_is_me(side, u):
        return (side == zb) & (yl + 2 * u == yh) & (yl == zb) & (c == yh // 2)

    barrier = pltpu.get_barrier_semaphore()

    def greet(dev):
        pl.semaphore_signal(barrier, inc=1, device_id=device(*dev), device_id_type=MESH)

    for dx, fy, fc in tensor:
        greet(tensor_dev(dx, fy, fc))
    for k, dy in column:
        greet(column_dev(k, dy))
    for dza, fc in depth[:-1]:
        greet(far(dza, fc))
    met = 15 + 7 + 4
    for i in range(2):
        for h in range(2):

            @pl.when(jnp.logical_not(hid_target_is_me(i, h)))
            def _():
                greet(hid_target(i, h))

    for side in range(2):
        for u in range(2):

            @pl.when(jnp.logical_not(hid_source_is_me(side, u)))
            def _():
                greet(hid_source(side, u))

    own_hop = jnp.where((yl == zb) & (yl == yh % 2) & (c == yh // 2), 1, 0)

    for load in loads[:3]:
        load.wait()
    rows = lax.broadcasted_iota(jnp.int32, (128, 128), 0)
    cols = lax.broadcasted_iota(jnp.int32, (128, 128), 1)
    causal = rows >= cols
    heads = ld_ref.shape[0]
    padded = jnp.concatenate([ld_ref[...], jnp.zeros((128 - heads, 128), F32)], axis=0)
    running_t = nt_dot(padded, causal.astype(F32), HIGHEST)
    running = running_t.T
    low = cols < MHEAD
    total = jnp.zeros((128, 128), F32)
    for p in range(heads // 2):
        xp = x_ref[:, p * 128 : (p + 1) * 128]
        zero = jnp.zeros_like(xp)
        both = jnp.concatenate([jnp.where(low, xp, zero), jnp.where(low, zero, xp)], axis=0)
        inner = nt_dot(dy_ref[:, p * 128 : (p + 1) * 128], both)
        for k in range(2):
            h = 2 * p + k
            gap = running[:, h : h + 1] - running_t[h : h + 1, :]
            decay = jnp.exp(jnp.where(causal, gap, -1e30))
            total = total + inner[:, k * 128 : (k + 1) * 128] * decay
    gram[0] = total

    for load in loads[3:]:
        load.wait()
    hid = hid_ref[...].astype(F32)
    gain = gain_ref[...].astype(F32).reshape(1, -1)
    scaled = hid * gain
    for k in range(4):
        ht[k] = scaled[:, k * 128 : (k + 1) * 128].T.astype(BF16)

    def row_of(column):
        return jnp.broadcast_to(column, (128, 128)).T[0:8, :]

    def column_of(row):
        return jnp.broadcast_to(row[0:1, :], (128, 128)).T

    sums[0] = row_of(jnp.sum(hid * hid, axis=1, keepdims=True))
    wall[c, za] = w_ref[pl.ds(pl.multiple_of(c * 128, 128), 128), :]

    pl.semaphore_wait(barrier, met + 8 - 2 * own_hop)

    gram_copy = remote(gram.at[0], gram.at[1], S_GRAM, sibling)
    gram_copy.start()

    sq_sibling = remote(sums.at[0], sums_in.at[0, 0], S_SQ, sibling)
    sq_sibling.start()

    def sq_copy(n):
        return remote(sums.at[1], sums_in.at[0, 1 + n], S_SQ + 1 + n, plane_dev(*plane[n]))

    def mean_copy(n):
        return remote(sums.at[2], sums_in.at[1, n], S_MEAN + n, tensor_dev(*tensor[n]))

    def hid_copy(i, h):
        lane = (2 * zb + yh // 2) * 128
        return remote(
            ht.at[2 * i + h],
            hall.at[yh % 2, x, :, pl.ds(pl.multiple_of(lane, 128), 128)],
            S_HID + 2 * i + h,
            hid_target(i, h),
            S_HID + 2 * zb + yh // 2,
        )

    def hid_arrival(side, u):
        lane = (2 * side + u) * 128
        return remote(
            ht.at[0],
            hall.at[yl, x, :, pl.ds(pl.multiple_of(lane, 128), 128)],
            S_HID + 2 * side + u,
            sibling,
        )

    for i in range(2):
        for h in range(2):

            @pl.when(jnp.logical_not(hid_target_is_me(i, h)))
            def _():
                hid_copy(i, h).start()

            @pl.when(hid_target_is_me(i, h))
            def _():
                lane = (2 * zb + yh // 2) * 128
                own = pltpu.make_async_copy(
                    ht.at[2 * i + h],
                    hall.at[yl, x, :, pl.ds(pl.multiple_of(lane, 128), 128)],
                    lsem,
                )
                own.start()
                own.wait()

    def w_copy(n):
        dza, fc = depth[n]
        core = (c + fc) % 2
        return remote(
            w_ref.at[pl.ds(pl.multiple_of(core * 128, 128), 128), :],
            wall.at[c, za],
            S_W + n,
            far(dza, fc),
        )

    def w_arrival(n):
        dza, fc = depth[n]
        return remote(
            w_ref.at[0:128, :], wall.at[(c + fc) % 2, (za + 4 - dza) % 4], S_W + n, sibling
        )

    for n in range(5):
        w_copy(n).start()

    def w_on(j):
        block = wall.at[j, (za + (1, 3)[j] + 2) % 4]
        return remote(block, block, S_W + 5 + j, far((1, 3)[j], 0))

    def w_on_arrival(j):
        block = wall.at[j, (za + 2) % 4]
        return remote(block, block, S_W + 5 + j, sibling)

    sq_sibling.wait_recv()
    sums[1] = sums[0] + sums_in[0, 0]
    for n in range(7):
        sq_copy(n).start()

    gram_copy.wait_recv()
    total = gram[0] + gram[1]
    bc = bc_ref[...].astype(F32)
    grad_b = nn_dot(total.T, bc[:, 128:], HIGHEST)
    grad_c = nn_dot(total, bc[:, :128], HIGHEST)
    dall[(c,) + seq(zb, yh)] = jnp.concatenate([grad_b, grad_c], axis=1).astype(BF16)

    def d_y(dy):
        block = dall.at[(c,) + seq(zb, yh)]
        return remote(block, block, S_DY + dy, column_dev(0, dy))

    def d_y_arrival(dy):
        block = dall.at[(c,) + seq(zb, (yh + 4 - dy) % 4)]
        return remote(block, block, S_DY + dy, sibling)

    def d_z(dy):
        if dy == 2:
            block = dall.at[(c,) + seq(1 - zb, yh)]
            return remote(block, block, S_DZ + dy, column_dev(0, 2))
        block = dall.at[(c,) + seq(zb, (yh + 4 - dy) % 4)]
        return remote(block, block, S_DZ + dy, column_dev(1, 0))

    def d_z_arrival(dy):
        block = dall.at[(c,) + seq(1 - zb, (yh + 4 - dy) % 4)]
        return remote(block, block, S_DZ + dy, sibling)

    def d_c(k, dy):
        block = dall.at[(c,) + seq((zb + k) % 2, (yh + 4 - dy) % 4)]
        return remote(block, block, S_DC + 4 * k + dy, sibling)

    def d_c_arrival(k, dy):
        block = dall.at[(1 - c,) + seq((zb + k) % 2, (yh + 4 - dy) % 4)]
        return remote(block, block, S_DC + 4 * k + dy, sibling)

    for dy in (1, 3):
        d_y(dy).start()
    d_z(0).start()
    d_c(0, 0).start()
    d_y(2).start()

    def h_block(k, sy, sx):
        lane = ((zb + k) % 2) * 256
        return hall.at[sy, sx, :, pl.ds(pl.multiple_of(lane, 128), 256)]

    def h_copy(k, n):
        dx, fy = plane[n]
        block = h_block(k, (yl + fy) % 2 if dx else yl, x)
        dev = (za, zb, yh, (x + dx) % 4, yl if dx else 1 - yl, c)
        return remote(block, block, S_HAG + 7 * k + n, dev)

    def h_arrival(k, n):
        sx, sy = plane_src(*plane[n])
        block = h_block(k, sy, sx)
        return remote(block, block, S_HAG + 7 * k + n, sibling)

    def hid_on(k):
        side = (zb + k) % 2
        for u in range(2):

            @pl.when(jnp.logical_not(hid_source_is_me(side, u)))
            def _():
                hid_arrival(side, u).wait_recv()

        for n in (3, 0, 1):
            h_copy(k, n).start()

    def hid_across(k):
        h_arrival(k, 3).wait_recv()
        for n in (4, 5):
            h_copy(k, n).start()

    def hid_far(k, fy):
        sx, sy = plane_src((1, 3)[k], fy)
        block = h_block(k, sy, sx)
        slot = S_HAG + 7 * k + 2 + 4 * fy
        return remote(block, block, slot, (za, zb, yh, (x + (1, 3)[k]) % 4, yl, c))

    def hid_relay(k, fy):
        h_arrival(k, k + 4 * fy).wait_recv()
        hid_far(k, fy).start()

    hid_on(0)
    hid_on(1)

    def d_on(dy):
        d_y_arrival(dy).wait_recv()
        if dy != 2:
            d_z(dy).start()
        d_c(0, dy).start()

    square = sums[1]
    for n in range(7):
        sq_copy(n).wait_recv()
        square = square + sums_in[0, 1 + n]
    mean_square = square * (1.0 / 8192.0) + EPSILON
    inv_root = lax.rsqrt(mean_square)
    inv[seq(zb, yh)] = inv_root

    def inv_copy(n):
        block = inv.at[seq(zb, yh)]
        return remote(block, block, S_INV + n, column_dev(*column[n]))

    def inv_arrival(n):
        k, dy = column[n]
        block = inv.at[seq((zb + k) % 2, (yh + 4 - dy) % 4)]
        return remote(block, block, S_INV + n, sibling)

    for n in range(7):
        inv_copy(n).start()

    d_on(1)
    d_on(3)
    for n in range(4):
        w_arrival(n).wait_recv()
    for j in range(2):
        w_on(j).start()
    d_z_arrival(0).wait_recv()
    d_z(2).start()
    d_c(1, 0).start()
    hid_across(0)
    hid_relay(0, 0)
    hid_relay(1, 0)
    d_on(2)
    hid_across(1)

    for dy in (0, 1, 3, 2):
        d_c_arrival(0, dy).wait_recv()

    def p_copy(k, n):
        dx, fy = plane[n]
        side = (zb + k) % 2
        relayed = k == 0 and (dx, fy) in ((1, 0), (3, 1))
        return remote(
            prelay.at[fy] if relayed else psend.at[side, (yl + fy) % 2, (x + dx) % 4],
            precv.at[side, yl, x],
            S_P + 7 * k + n,
            plane_dev(dx, fy),
        )

    def p_arrival(k, n):
        sx, sy = plane_src(*plane[n])
        block = precv.at[(zb + k) % 2, sy, sx]
        return remote(block, block, S_P + 7 * k + n, sibling)

    def terms(k, dza):
        side, tx = (zb + k) % 2, (za + dza) % 4
        for py in range(2):
            out = nt_dot(dall[0, py, side].reshape(256, 256), wall[0, tx])
            out = out + nt_dot(dall[1, py, side].reshape(256, 256), wall[1, tx])
            psend[side, py, tx] = out.astype(BF16)

    def p_far(fy):
        block = psend.at[zb, (yl + fy) % 2, (x + 2) % 4]
        dev = (za, zb, yh, (x + (1, 3)[fy]) % 4, yl, c)
        return remote(block, prelay.at[fy], S_P + 2 + 4 * fy, dev)

    def p_relay(fy):
        p_far(fy).wait_recv()
        to = (yl + fy) % 2, (x + (1, 3)[fy]) % 4
        own = psend[(zb,) + to].astype(F32)
        prelay[fy] = (own + prelay[fy].astype(F32)).astype(BF16)
        p_copy(0, 5 * fy).start()

    def p_start(k, dza):
        for n, (dx, fy) in enumerate(plane):
            if (dx, fy) in ((1, 0), (3, 1)):
                continue

            @pl.when((x + dx) % 4 == (za + dza) % 4)
            def _():
                if dx == 2:
                    p_far(fy).start()
                else:
                    p_copy(k, n).start()

    w_arrival(4).wait_recv()
    terms(0, 0)
    p_start(0, 0)
    terms(0, 1)
    p_start(0, 1)
    terms(0, 3)
    p_start(0, 3)
    hid_relay(0, 1)
    for j in range(2):
        w_on_arrival(j).wait_recv()
    terms(0, 2)
    p_start(0, 2)
    hid_relay(1, 1)
    for dy in (1, 3, 2):
        d_z_arrival(dy).wait_recv()
        d_c(1, dy).start()
    for dy in (0, 1, 3, 2):
        d_c_arrival(1, dy).wait_recv()
    for dza in range(4):
        terms(1, dza)

    def g_copy(d, j):
        dza = (1, 3)[d]
        dev = ((za + dza) % 4, zb, yh, x, yl, j)
        return remote(
            gsend.at[(za + dza) % 4, j], grecv.at[za, c], S_G + 2 * d + j, dev, S_G + 2 * d + c
        )

    def g_arrival(d, h):
        block = grecv.at[(za + (3, 1)[d]) % 4, h]
        return remote(block, block, S_G + 2 * d + h, sibling)

    def g_sibling():
        return remote(gsend.at[za, 1 - c], grecv.at[za, c], S_G + 4, sibling)

    def g_relay(j):
        return remote(
            gsend.at[(za + 2) % 4, j], grelay.at[j], S_G + 5 + j, far((1, 3)[j], 0)
        )

    for n in range(7):
        inv_arrival(n).wait_recv()
    inv_rows = [
        jnp.concatenate([inv[sy, side, u][0:1, :] for side in range(2) for u in range(2)], axis=1)
        for sy in range(2)
    ]
    inv_rows = [inv_rows[sy] * (1.0 / 64.0) for sy in range(2)]
    own_inv = jnp.where(yl == 0, inv_rows[0], inv_rows[1])
    other_inv = jnp.where(yl == 0, inv_rows[1], inv_rows[0])

    def scale(dx, fy):
        sx, sy = plane_src(dx, fy)
        row = other_inv if fy else own_inv
        hscaled[sy, sx] = (hall[sy, sx].astype(F32) * row).astype(BF16)

    p_relay(0)
    p_relay(1)

    scale(0, 0)
    scale(0, 1)
    for n in (0, 1, 4, 5, 2, 6):
        for k in range(2):
            if n % 4 != k:
                h_arrival(k, n).wait_recv()
        scale(*plane[n])
    eye = (rows == cols).astype(F32)
    for py in range(2):
        for side in range(2):
            for u in range(2):
                part = slice(u * 128, (u + 1) * 128)
                lane = (2 * side + u) * 128
                prod = jnp.zeros((128, 128), F32)
                for f in range(4):
                    prod = prod + nn_dot(
                        psend[side, py, f, part, :], hall[py, f, :, lane : lane + 128]
                    )
                row = jnp.sum(prod * eye, axis=0, keepdims=True)
                dots[py, side, u] = jnp.broadcast_to(row, (8, 128))

    def dot_copy(n):
        k, dy = column[n]
        block = dots.at[seq((zb + k) % 2, (yh + dy) % 4)]
        return remote(block, dots_in.at[n], S_DOT + n, column_dev(k, dy))

    for n in range(7):
        dot_copy(n).start()
    for n in range(7):
        p_copy(1, n).start()

    def g_terms(first, count, j):
        rows = [hscaled[sy, pl.ds(first, count)].reshape(count * 128, 512) for sy in range(2)]
        out = nn_dot(rows[0], dall[j, 0].reshape(512, 256))
        out = out + nn_dot(rows[1], dall[j, 1].reshape(512, 256))
        gsend[pl.ds(first, count), j] = out.astype(BF16).reshape(count, 128, 256)

    for j in range(2):
        g_terms((za + 2) % 4, 1, j)
        g_relay(j).start()
    for j in range(2):
        g_terms((za + (3, 1)[j]) % 4, 1, j)
        g_copy(1 - j, j).start()
    for j in range(2):
        g_terms((za + (1, 3)[j]) % 4, 1, j)
        g_terms(za, 1, j)
    g_sibling().start()

    def q_copy(k, u):
        side = (zb + k) % 2
        return remote(
            rsum.at[side, u],
            qrecv.at[yh % 2, c],
            S_Q + 2 * k + u,
            hid_source(side, u),
            S_Q + 2 * (yh % 2) + c,
        )

    def owners(k):
        side = (zb + k) % 2
        arrivals = (1, 4, 3, 0, 5) if k == 0 else range(7)
        for n in arrivals:
            p_arrival(k, n).wait_recv()
        acc = psend[side, yl, x].astype(F32)
        for n in arrivals:
            sx, sy = plane_src(*plane[n])
            acc = acc + precv[side, sy, sx].astype(F32)
        rsum[side] = acc.astype(BF16).reshape(2, 128, 128)
        for u in range(2):

            @pl.when(jnp.logical_not(hid_source_is_me(side, u)))
            def _():
                q_copy(k, u).start()

            @pl.when(hid_source_is_me(side, u))
            def _():
                own = pltpu.make_async_copy(rsum.at[side, u], qrecv.at[yh % 2, c], lsem)
                own.start()
                own.wait()

    for n in range(7):
        dot_copy(n).wait_recv()
    value = dots[seq(zb, yh)]
    for n in range(7):
        value = value + dots_in[n]
    sums[2] = value
    for n in range(15):
        mean_copy(n).start()
    for j in range(2):
        g_relay(j).wait_recv()
        to = (za + (1, 3)[j]) % 4
        gsend[to, j] = (gsend[to, j].astype(F32) + grelay[j].astype(F32)).astype(BF16)
        g_copy(j, j).start()

    owners(0)
    owners(1)

    g_sibling().wait_recv()
    for h in range(2):
        for d in range(2):
            g_arrival(d, h).wait_recv()
    grecv[za, c] = gsend[za, c]
    for h in range(2):
        acc = grecv[za, h].astype(F32)
        for d in range(2):
            acc = acc + grecv[(za + (3, 1)[d]) % 4, h].astype(F32)
        wgrad_ref[h * 128 : (h + 1) * 128, :] = acc.astype(BF16)

    wgrad_out = pltpu.make_async_copy(wgrad_ref, wgrad_hbm, isem.at[7])
    wgrad_out.start()
    dot = sums[2]
    for n in range(15):
        mean_copy(n).wait_recv()
        dot = dot + sums_in[1, n]
    factor = column_of(dot * (1.0 / 8192.0) / mean_square)
    inv_column = column_of(inv_root)
    for i in range(2):
        for h in range(2):

            @pl.when(jnp.logical_not(hid_target_is_me(i, h)))
            def _():
                remote(rsum.at[0, 0], qrecv.at[i, h], S_Q + 2 * i + h, sibling).wait_recv()

    for i in range(2):
        for h in range(2):
            k = 2 * i + h
            part = slice(k * 128, (k + 1) * 128)
            grad = qrecv[i, h].astype(F32) * gain[:, part]
            igrad_ref[:, part] = ((grad - hid[:, part] * factor) * inv_column).astype(BF16)

    igrad_out = pltpu.make_async_copy(igrad_ref, igrad_hbm, isem.at[8])
    igrad_out.start()

    for i in range(2):
        for h in range(2):

            @pl.when(jnp.logical_not(hid_target_is_me(i, h)))
            def _():
                hid_copy(i, h).wait_send()

    for k in range(2):
        for u in range(2):

            @pl.when(jnp.logical_not(hid_source_is_me((zb + k) % 2, u)))
            def _():
                q_copy(k, u).wait_send()

    sq_sibling.wait_send()
    for n in range(7):
        sq_copy(n).wait_send()
    for n in range(15):
        mean_copy(n).wait_send()
    gram_copy.wait_send()
    for n in range(5):
        w_copy(n).wait_send()
    g_sibling().wait_send()
    for j in range(2):
        w_on(j).wait_send()
        g_relay(j).wait_send()
        for d in range(2):
            g_copy(d, j).wait_send()
    for n in range(7):
        for k in range(2):
            if n % 4 != 2:
                h_copy(k, n).wait_send()
            else:
                hid_far(k, n // 4).wait_send()
        if n % 4 != 2:
            p_copy(0, n).wait_send()
        else:
            p_far(n // 4).wait_send()
        p_copy(1, n).wait_send()
        inv_copy(n).wait_send()
        dot_copy(n).wait_send()
    for dy in range(4):
        if dy:
            d_y(dy).wait_send()
        d_z(dy).wait_send()
        d_c(0, dy).wait_send()
        d_c(1, dy).wait_send()
    wgrad_out.wait()
    igrad_out.wait()


def hand_over(igrad_ref, wgrad_ref, igrad_out, wgrad_out, igrad, wgrad, sem):
    ins = [
        pltpu.make_async_copy(igrad_ref, igrad, sem.at[0]),
        pltpu.make_async_copy(wgrad_ref, wgrad, sem.at[1]),
    ]
    outs = [
        pltpu.make_async_copy(igrad, igrad_out, sem.at[2]),
        pltpu.make_async_copy(wgrad, wgrad_out, sem.at[3]),
    ]
    for copy in ins:
        copy.start()
    for first, second in zip(ins, outs):
        first.wait()
        second.start()
    for copy in outs:
        copy.wait()


def shards(hidden, gain, proj_weight, b_c, ssm_x, dy, log_decay):
    hbm = pl.BlockSpec(memory_space=pl.ANY)
    grads = pl.pallas_call(
        kernel,
        out_shape=(
            jax.ShapeDtypeStruct(hidden.shape, BF16),
            jax.ShapeDtypeStruct(proj_weight.shape, BF16),
        ),
        in_specs=[hbm] * 7,
        out_specs=(hbm, hbm),
        scratch_shapes=[
            pltpu.VMEM(hidden.shape, BF16),
            pltpu.VMEM(proj_weight.shape, BF16),
            pltpu.VMEM(hidden.shape, BF16),
            pltpu.VMEM(gain.shape, BF16),
            pltpu.VMEM(proj_weight.shape, BF16),
            pltpu.VMEM(b_c.shape, BF16),
            pltpu.VMEM(ssm_x.shape, BF16),
            pltpu.VMEM(dy.shape, BF16),
            pltpu.VMEM(log_decay.shape[::-1], F32),
            pltpu.VMEM((4, 128, 128), BF16),
            pltpu.VMEM((2, 4, 128, 512), BF16),
            pltpu.VMEM((2, 4, 128, 512), BF16),
            pltpu.VMEM((2, 4, 128, 256), BF16),
            pltpu.VMEM((3, 8, 128), F32),
            pltpu.VMEM((2, 15, 8, 128), F32),
            pltpu.VMEM((2, 2, 2, 8, 128), F32),
            pltpu.VMEM((2, 2, 2, 8, 128), F32),
            pltpu.VMEM((7, 8, 128), F32),
            pltpu.VMEM((2, 128, 128), F32),
            pltpu.VMEM((2, 2, 2, 2, 128, 256), BF16),
            pltpu.VMEM((2, 2, 4, 256, 128), BF16),
            pltpu.VMEM((2, 2, 4, 256, 128), BF16),
            pltpu.VMEM((2, 2, 128, 128), BF16),
            pltpu.VMEM((2, 2, 128, 128), BF16),
            pltpu.VMEM((4, 2, 128, 256), BF16),
            pltpu.VMEM((4, 2, 128, 256), BF16),
            pltpu.VMEM((2, 128, 256), BF16),
            pltpu.VMEM((2, 256, 128), BF16),
            pltpu.SemaphoreType.DMA((N_SLOTS,)),
            pltpu.SemaphoreType.DMA((N_SLOTS,)),
            pltpu.SemaphoreType.DMA,
            pltpu.SemaphoreType.DMA((9,)),
        ],
        compiler_params=pltpu.CompilerParams(
            collective_id=0, has_side_effects=True, vmem_limit_bytes=63 * 1024 * 1024
        ),
        name="projection_backward",
    )(hidden, gain, proj_weight, b_c, ssm_x, dy, log_decay.T)
    return pl.pallas_call(
        hand_over,
        out_shape=tuple(jax.ShapeDtypeStruct(grad.shape, grad.dtype) for grad in grads),
        in_specs=[hbm] * 2,
        out_specs=(hbm, hbm),
        scratch_shapes=[
            pltpu.VMEM(hidden.shape, BF16),
            pltpu.VMEM(proj_weight.shape, BF16),
            pltpu.SemaphoreType.DMA((4,)),
        ],
        compiler_params=pltpu.CompilerParams(vmem_limit_bytes=63 * 1024 * 1024),
        name="hand_over",
    )(*grads)


def solution(mesh):
    return jax.shard_map(
        shards,
        mesh=mesh,
        in_specs=(
            P("dp", "tensor"),
            P("tensor"),
            P("dp", "tensor"),
            P("dp", "tensor"),
            P("dp", "tensor"),
            P("dp", "tensor"),
            P("dp", "tensor"),
        ),
        out_specs=(P("dp", "tensor"), P("dp", "tensor")),
        check_vma=False,
    )
```

```python
import jax
import jax.numpy as jnp
from jax import lax
from jax.experimental import pallas as pl
from jax.experimental.pallas import tpu as pltpu
from jax.sharding import PartitionSpec as P

MHEAD = 64
EPSILON = 1e-05
MESH = pl.DeviceIdType.MESH
F32 = jnp.float32
BF16 = jnp.bfloat16
HIGHEST = lax.Precision.HIGHEST


def device(za, zb, yh, x, yl, c):
    return {"dp": (za * 2 + zb) * 4 + yh, "tensor": x * 4 + yl * 2 + c}


def nt_dot(a, b, precision=None):
    return lax.dot_general(
        a, b, (((1,), (1,)), ((), ())), preferred_element_type=F32, precision=precision
    )


def nn_dot(a, b, precision=None):
    return lax.dot_general(
        a, b, (((1,), (0,)), ((), ())), preferred_element_type=F32, precision=precision
    )


class Slots:
    def __init__(self):
        self.count = 0

    def take(self, n):
        first = self.count
        self.count += n
        return first


SLOTS = Slots()
S_HID = SLOTS.take(4)
S_HAG = SLOTS.take(14)
S_W = SLOTS.take(7)
S_SQ = SLOTS.take(8)
S_INV = SLOTS.take(8)
S_GRAM = SLOTS.take(1)
S_DY = SLOTS.take(4)
S_DZ = SLOTS.take(4)
S_DC = SLOTS.take(8)
S_P = SLOTS.take(14)
S_Q = SLOTS.take(4)
S_G = SLOTS.take(3)
S_GIN = SLOTS.take(4)
S_GON = SLOTS.take(4)
S_DOT = SLOTS.take(8)
S_MEAN = SLOTS.take(15)
N_SLOTS = SLOTS.count


def kernel(
    hid_hbm,
    gain_hbm,
    w_hbm,
    bc_hbm,
    x_hbm,
    dy_hbm,
    ld_hbm,
    igrad_hbm,
    wgrad_hbm,
    igrad_ref,
    wgrad_ref,
    hid_ref,
    gain_ref,
    w_ref,
    bc_ref,
    x_ref,
    dy_ref,
    ld_ref,
    ht,
    hall,
    hscaled,
    wall,
    sums,
    sums_in,
    inv,
    dots,
    dots_in,
    gram,
    dall,
    psend,
    precv,
    rsum,
    qrecv,
    gsend,
    grecv,
    grelay,
    prelay,
    ssem,
    rsem,
    lsem,
    isem,
):
    loads = [
        pltpu.make_async_copy(src, dst, isem.at[n])
        for n, (src, dst) in enumerate(
            (
                (ld_hbm, ld_ref),
                (x_hbm, x_ref),
                (dy_hbm, dy_ref),
                (hid_hbm, hid_ref),
                (gain_hbm, gain_ref),
                (w_hbm, w_ref),
                (bc_hbm, bc_ref),
            )
        )
    ]
    for load in loads:
        load.start()

    dp = lax.axis_index("dp")
    ten = lax.axis_index("tensor")
    z, yh = dp // 4, dp % 4
    za, zb = z // 2, z % 2
    x, yl, c = ten // 4, (ten // 2) % 2, ten % 2

    def remote(src, dst, slot, dev, rslot=None):
        rslot = slot if rslot is None else rslot
        return pltpu.make_async_remote_copy(
            src_ref=src,
            dst_ref=dst,
            send_sem=ssem.at[slot],
            recv_sem=rsem.at[rslot],
            device_id=device(*dev),
            device_id_type=MESH,
        )

    sibling = (za, zb, yh, x, yl, 1 - c)
    plane = [(1, 0), (3, 0), (2, 0), (0, 1), (1, 1), (3, 1), (2, 1)]
    column = [(0, 1), (0, 3), (0, 2), (1, 0), (1, 1), (1, 3), (1, 2)]
    depth = [(dza, fc) for dza in (1, 3) for fc in range(2)] + [(0, 1)]
    tensor = [(0, 0, 1)] + [(dx, fy, fc) for fc in range(2) for dx, fy in plane]

    def plane_dev(dx, fy):
        return (za, zb, yh, (x + dx) % 4, (yl + fy) % 2, c)

    def plane_src(dx, fy):
        return (x + 4 - dx) % 4, (yl + fy) % 2

    def tensor_dev(dx, fy, fc):
        return (za, zb, yh, (x + dx) % 4, (yl + fy) % 2, (c + fc) % 2)

    def column_dev(k, dy):
        return (za, (zb + k) % 2, (yh + dy) % 4, x, yl, c)

    def far(dza, fc):
        return ((za + dza) % 4, zb, yh, x, yl, (c + fc) % 2)

    def seq(side, y):
        return (y % 2, side, y // 2)

    def hid_target(i, h):
        return (za, yl, 2 * c + i, x, yh % 2, h)

    def hid_target_is_me(i, h):
        return (yl == zb) & (yh == 2 * c + i) & (yl == yh % 2) & (c == h)

    def hid_source(side, u):
        return (za, side, yl + 2 * u, x, zb, yh // 2)

    def hid_source_is_me(side, u):
        return (side == zb) & (yl + 2 * u == yh) & (yl == zb) & (c == yh // 2)

    barrier = pltpu.get_barrier_semaphore()

    def greet(dev):
        pl.semaphore_signal(barrier, inc=1, device_id=device(*dev), device_id_type=MESH)

    for dx, fy, fc in tensor:
        greet(tensor_dev(dx, fy, fc))
    for k, dy in column:
        greet(column_dev(k, dy))
    for dza, fc in depth[:-1]:
        greet(far(dza, fc))
    met = 15 + 7 + 4
    for i in range(2):
        for h in range(2):

            @pl.when(jnp.logical_not(hid_target_is_me(i, h)))
            def _():
                greet(hid_target(i, h))

    for side in range(2):
        for u in range(2):

            @pl.when(jnp.logical_not(hid_source_is_me(side, u)))
            def _():
                greet(hid_source(side, u))

    own_hop = jnp.where((yl == zb) & (yl == yh % 2) & (c == yh // 2), 1, 0)

    for load in loads[:3]:
        load.wait()
    rows = lax.broadcasted_iota(jnp.int32, (128, 128), 0)
    cols = lax.broadcasted_iota(jnp.int32, (128, 128), 1)
    causal = rows >= cols
    heads = ld_ref.shape[0]
    padded = jnp.concatenate([ld_ref[...], jnp.zeros((128 - heads, 128), F32)], axis=0)
    running_t = nt_dot(padded, causal.astype(F32), HIGHEST)
    running = running_t.T
    low = cols < MHEAD
    total = jnp.zeros((128, 128), F32)
    for p in range(heads // 2):
        xp = x_ref[:, p * 128 : (p + 1) * 128]
        zero = jnp.zeros_like(xp)
        both = jnp.concatenate([jnp.where(low, xp, zero), jnp.where(low, zero, xp)], axis=0)
        inner = nt_dot(dy_ref[:, p * 128 : (p + 1) * 128], both)
        for k in range(2):
            h = 2 * p + k
            gap = running[:, h : h + 1] - running_t[h : h + 1, :]
            decay = jnp.exp(jnp.where(causal, gap, -1e30))
            total = total + inner[:, k * 128 : (k + 1) * 128] * decay
    gram[0] = total

    for load in loads[3:]:
        load.wait()
    hid = hid_ref[...].astype(F32)
    gain = gain_ref[...].astype(F32).reshape(1, -1)
    scaled = hid * gain
    for k in range(4):
        ht[k] = scaled[:, k * 128 : (k + 1) * 128].T.astype(BF16)

    def row_of(column):
        return jnp.broadcast_to(column, (128, 128)).T[0:1, :]

    def column_of(row):
        return jnp.broadcast_to(row[0:1, :], (128, 128)).T

    sums[0] = row_of(jnp.sum(hid * hid, axis=1, keepdims=True))
    wall[c, za] = w_ref[pl.ds(pl.multiple_of(c * 128, 128), 128), :]

    pl.semaphore_wait(barrier, met + 8 - 2 * own_hop)

    gram_copy = remote(gram.at[0], gram.at[1], S_GRAM, sibling)
    gram_copy.start()

    sq_sibling = remote(sums.at[0], sums_in.at[0, 0], S_SQ, sibling)
    sq_sibling.start()

    def sq_copy(n):
        return remote(sums.at[1], sums_in.at[0, 1 + n], S_SQ + 1 + n, plane_dev(*plane[n]))

    def mean_copy(n):
        return remote(sums.at[2], sums_in.at[1, n], S_MEAN + n, tensor_dev(*tensor[n]))

    def hid_copy(i, h):
        lane = (2 * zb + yh // 2) * 128
        return remote(
            ht.at[2 * i + h],
            hall.at[yh % 2, x, :, pl.ds(pl.multiple_of(lane, 128), 128)],
            S_HID + 2 * i + h,
            hid_target(i, h),
            S_HID + 2 * zb + yh // 2,
        )

    def hid_arrival(side, u):
        lane = (2 * side + u) * 128
        return remote(
            ht.at[0],
            hall.at[yl, x, :, pl.ds(pl.multiple_of(lane, 128), 128)],
            S_HID + 2 * side + u,
            sibling,
        )

    for i in range(2):
        for h in range(2):

            @pl.when(jnp.logical_not(hid_target_is_me(i, h)))
            def _():
                hid_copy(i, h).start()

            @pl.when(hid_target_is_me(i, h))
            def _():
                lane = (2 * zb + yh // 2) * 128
                own = pltpu.make_async_copy(
                    ht.at[2 * i + h],
                    hall.at[yl, x, :, pl.ds(pl.multiple_of(lane, 128), 128)],
                    lsem,
                )
                own.start()
                own.wait()

    def w_copy(n):
        dza, fc = depth[n]
        core = (c + fc) % 2
        return remote(
            w_ref.at[pl.ds(pl.multiple_of(core * 128, 128), 128), :],
            wall.at[c, za],
            S_W + n,
            far(dza, fc),
        )

    def w_arrival(n):
        dza, fc = depth[n]
        return remote(
            w_ref.at[0:128, :], wall.at[(c + fc) % 2, (za + 4 - dza) % 4], S_W + n, sibling
        )

    for n in range(5):
        w_copy(n).start()

    def w_on(j):
        block = wall.at[j, (za + (1, 3)[j] + 2) % 4]
        return remote(block, block, S_W + 5 + j, far((1, 3)[j], 0))

    def w_on_arrival(j):
        block = wall.at[j, (za + 2) % 4]
        return remote(block, block, S_W + 5 + j, sibling)

    sq_sibling.wait_recv()
    sums[1] = sums[0] + sums_in[0, 0]
    for n in range(7):
        sq_copy(n).start()

    gram_copy.wait_recv()
    total = gram[0] + gram[1]
    bc = bc_ref[...].astype(F32)
    grad_b = nn_dot(total.T, bc[:, 128:], HIGHEST)
    grad_c = nn_dot(total, bc[:, :128], HIGHEST)
    dall[(c,) + seq(zb, yh)] = jnp.concatenate([grad_b, grad_c], axis=1).astype(BF16)

    def d_y(dy):
        block = dall.at[(c,) + seq(zb, yh)]
        return remote(block, block, S_DY + dy, column_dev(0, dy))

    def d_far(dy):
        half = slice(0, 64) if dy == 1 else slice(64, 128)
        block = dall.at[(c,) + seq(zb, (yh + 4 - dy) % 4) + (half,)]
        return remote(block, block, S_DY + dy - 1, column_dev(0, dy))

    def d_far_arrival(dy):
        half = slice(0, 64) if dy == 1 else slice(64, 128)
        block = dall.at[(c,) + seq(zb, (yh + 2) % 4) + (half,)]
        return remote(block, block, S_DY + dy - 1, sibling)

    def d_y_arrival(dy):
        block = dall.at[(c,) + seq(zb, (yh + 4 - dy) % 4)]
        return remote(block, block, S_DY + dy, sibling)

    def d_z(dy):
        if dy == 2:
            block = dall.at[(c,) + seq(1 - zb, yh)]
            return remote(block, block, S_DZ + dy, column_dev(0, 2))
        block = dall.at[(c,) + seq(zb, (yh + 4 - dy) % 4)]
        return remote(block, block, S_DZ + dy, column_dev(1, 0))

    def d_z_arrival(dy):
        block = dall.at[(c,) + seq(1 - zb, (yh + 4 - dy) % 4)]
        return remote(block, block, S_DZ + dy, sibling)

    def d_c(k, dy):
        block = dall.at[(c,) + seq((zb + k) % 2, (yh + 4 - dy) % 4)]
        return remote(block, block, S_DC + 4 * k + dy, sibling)

    def d_c_arrival(k, dy):
        block = dall.at[(1 - c,) + seq((zb + k) % 2, (yh + 4 - dy) % 4)]
        return remote(block, block, S_DC + 4 * k + dy, sibling)

    for dy in (1, 3):
        d_y(dy).start()
    d_z(0).start()
    d_c(0, 0).start()

    def h_block(k, sy, sx):
        lane = ((zb + k) % 2) * 256
        return hall.at[sy, sx, :, pl.ds(pl.multiple_of(lane, 128), 256)]

    def h_copy(k, n):
        dx, fy = plane[n]
        block = h_block(k, (yl + fy) % 2 if dx else yl, x)
        dev = (za, zb, yh, (x + dx) % 4, yl if dx else 1 - yl, c)
        return remote(block, block, S_HAG + 7 * k + n, dev)

    def h_arrival(k, n):
        sx, sy = plane_src(*plane[n])
        block = h_block(k, sy, sx)
        return remote(block, block, S_HAG + 7 * k + n, sibling)

    def hid_on(k):
        side = (zb + k) % 2
        for u in range(2):

            @pl.when(jnp.logical_not(hid_source_is_me(side, u)))
            def _():
                hid_arrival(side, u).wait_recv()

        for n in (3, 0, 1):
            h_copy(k, n).start()

    def hid_across(k):
        h_arrival(k, 3).wait_recv()
        for n in (4, 5):
            h_copy(k, n).start()

    def hid_far(k, fy):
        sx, sy = plane_src((1, 3)[k], fy)
        block = h_block(k, sy, sx)
        slot = S_HAG + 7 * k + 2 + 4 * fy
        return remote(block, block, slot, (za, zb, yh, (x + (1, 3)[k]) % 4, yl, c))

    def hid_relay(k, fy):
        h_arrival(k, k + 4 * fy).wait_recv()
        hid_far(k, fy).start()

    hid_on(0)
    hid_on(1)

    def d_on(dy):
        if dy == 2:
            d_far_arrival(1).wait_recv()
            d_far_arrival(3).wait_recv()
        else:
            d_y_arrival(dy).wait_recv()
            d_far(dy).start()
            d_z(dy).start()
        d_c(0, dy).start()

    square = sums[1]
    for n in range(7):
        sq_copy(n).wait_recv()
        square = square + sums_in[0, 1 + n]
    mean_square = square * (1.0 / 8192.0) + EPSILON
    inv_root = lax.rsqrt(mean_square)
    inv[seq(zb, yh)] = inv_root

    def inv_copy(n):
        block = inv.at[seq(zb, yh)]
        return remote(block, block, S_INV + n, column_dev(*column[n]))

    def inv_arrival(n):
        k, dy = column[n]
        block = inv.at[seq((zb + k) % 2, (yh + 4 - dy) % 4)]
        return remote(block, block, S_INV + n, sibling)

    for n in range(7):
        inv_copy(n).start()

    d_on(1)
    d_on(3)
    for n in range(4):
        w_arrival(n).wait_recv()
    for j in range(2):
        w_on(j).start()
    d_z_arrival(0).wait_recv()
    d_z(2).start()
    d_c(1, 0).start()
    hid_across(0)
    hid_relay(0, 0)
    hid_relay(1, 0)
    d_on(2)
    hid_across(1)

    for dy in (0, 1, 3, 2):
        d_c_arrival(0, dy).wait_recv()

    def p_copy(k, n):
        dx, fy = plane[n]
        side = (zb + k) % 2
        relayed = k == 0 and (dx, fy) in ((1, 0), (3, 1))
        return remote(
            prelay.at[fy] if relayed else psend.at[side, (yl + fy) % 2, (x + dx) % 4],
            precv.at[side, yl, x],
            S_P + 7 * k + n,
            plane_dev(dx, fy),
        )

    def p_arrival(k, n):
        sx, sy = plane_src(*plane[n])
        block = precv.at[(zb + k) % 2, sy, sx]
        return remote(block, block, S_P + 7 * k + n, sibling)

    def terms(k, dza):
        side, tx = (zb + k) % 2, (za + dza) % 4
        for py in range(2):
            out = nt_dot(dall[0, py, side].reshape(256, 256), wall[0, tx])
            out = out + nt_dot(dall[1, py, side].reshape(256, 256), wall[1, tx])
            psend[side, py, tx] = out.astype(BF16)

    def p_far(fy):
        block = psend.at[zb, (yl + fy) % 2, (x + 2) % 4]
        dev = (za, zb, yh, (x + (1, 3)[fy]) % 4, yl, c)
        return remote(block, prelay.at[fy], S_P + 2 + 4 * fy, dev)

    def p_relay(fy):
        p_far(fy).wait_recv()
        to = (yl + fy) % 2, (x + (1, 3)[fy]) % 4
        own = psend[(zb,) + to].astype(F32)
        prelay[fy] = (own + prelay[fy].astype(F32)).astype(BF16)
        p_copy(0, 5 * fy).start()

    def p_start(k, dza):
        for n, (dx, fy) in enumerate(plane):
            if (dx, fy) in ((1, 0), (3, 1)):
                continue

            @pl.when((x + dx) % 4 == (za + dza) % 4)
            def _():
                if dx == 2:
                    p_far(fy).start()
                else:
                    p_copy(k, n).start()

    w_arrival(4).wait_recv()
    terms(0, 0)
    p_start(0, 0)
    terms(0, 1)
    p_start(0, 1)
    terms(0, 3)
    p_start(0, 3)
    hid_relay(0, 1)
    for j in range(2):
        w_on_arrival(j).wait_recv()
    terms(0, 2)
    p_start(0, 2)
    hid_relay(1, 1)
    for dy in (1, 3, 2):
        d_z_arrival(dy).wait_recv()
        d_c(1, dy).start()
    for dy in (0, 1, 3, 2):
        d_c_arrival(1, dy).wait_recv()
    for dza in range(4):
        terms(1, dza)

    def g_dev(dza, j):
        return ((za + dza) % 4, zb, yh, x, yl, j)

    def g_copy(j):
        dza = (3, 1)[j]
        return remote(
            gsend.at[(za + dza) % 4, j], grecv.at[za, c], S_G + j, g_dev(dza, j), S_G + c
        )

    def g_arrival(h):
        block = grecv.at[jnp.where(c == 0, (za + 1) % 4, (za + 3) % 4), h]
        return remote(block, block, S_G + h, sibling)

    def g_sibling():
        return remote(gsend.at[za, 1 - c], grecv.at[za, c], S_G + 2, sibling)

    def g_relay(j, part):
        half = slice(part * 64, part * 64 + 64)
        return remote(
            gsend.at[(za + 2) % 4, j, half],
            grelay.at[j, half],
            S_GIN + 2 * j + part,
            g_dev((1, 3)[j], c),
        )

    def g_on(j, part):
        dza = (1, 3)[j]
        half = slice(part * 64, part * 64 + 64)
        return remote(
            gsend.at[(za + dza) % 4, j, half],
            grecv.at[za, c, half],
            S_GON + 2 * j + part,
            g_dev(dza, j),
            S_GON + 2 * c + part,
        )

    def g_on_arrival(h, part):
        half = slice(part * 64, part * 64 + 64)
        block = grecv.at[jnp.where(c == 0, (za + 3) % 4, (za + 1) % 4), h, half]
        return remote(block, block, S_GON + 2 * h + part, sibling)

    for n in range(7):
        inv_arrival(n).wait_recv()
    inv_rows = [
        jnp.concatenate([inv[sy, side, u][0:1, :] for side in range(2) for u in range(2)], axis=1)
        for sy in range(2)
    ]
    inv_rows = [inv_rows[sy] * (1.0 / 64.0) for sy in range(2)]
    own_inv = jnp.where(yl == 0, inv_rows[0], inv_rows[1])
    other_inv = jnp.where(yl == 0, inv_rows[1], inv_rows[0])

    def scale(dx, fy):
        sx, sy = plane_src(dx, fy)
        row = other_inv if fy else own_inv
        hscaled[sy, sx] = (hall[sy, sx].astype(F32) * row).astype(BF16)

    p_relay(0)
    p_relay(1)

    scale(0, 0)
    scale(0, 1)
    for n in (0, 1, 4, 5, 2, 6):
        for k in range(2):
            if n % 4 != k:
                h_arrival(k, n).wait_recv()
        scale(*plane[n])
    eye = (rows == cols).astype(F32)
    for py in range(2):
        for side in range(2):
            for u in range(2):
                part = slice(u * 128, (u + 1) * 128)
                lane = (2 * side + u) * 128
                prod = jnp.zeros((128, 128), F32)
                for f in range(4):
                    prod = prod + nn_dot(
                        psend[side, py, f, part, :], hall[py, f, :, lane : lane + 128]
                    )
                row = jnp.sum(prod * eye, axis=0, keepdims=True)
                dots[py, side, u] = row

    def dot_copy(n):
        k, dy = column[n]
        block = dots.at[seq((zb + k) % 2, (yh + dy) % 4)]
        return remote(block, dots_in.at[n], S_DOT + n, column_dev(k, dy))

    for n in range(7):
        dot_copy(n).start()
    for n in range(7):
        p_copy(1, n).start()

    def g_terms(first, count, j):
        rows = [hscaled[sy, pl.ds(first, count)].reshape(count * 128, 512) for sy in range(2)]
        out = nn_dot(rows[0], dall[j, 0].reshape(512, 256))
        out = out + nn_dot(rows[1], dall[j, 1].reshape(512, 256))
        gsend[pl.ds(first, count), j] = out.astype(BF16).reshape(count, 128, 256)

    for j in range(2):
        g_terms((za + 2) % 4, 1, j)
        g_relay(j, 0).start()
    for j in range(2):
        g_relay(j, 1).start()
    for j in range(2):
        g_terms((za + (3, 1)[j]) % 4, 1, j)
        g_copy(j).start()
    for j in range(2):
        g_terms((za + (1, 3)[j]) % 4, 1, j)
        g_terms(za, 1, j)
    g_sibling().start()

    def q_copy(k, u):
        side = (zb + k) % 2
        return remote(
            rsum.at[side, u],
            qrecv.at[yh % 2, c],
            S_Q + 2 * k + u,
            hid_source(side, u),
            S_Q + 2 * (yh % 2) + c,
        )

    def owners(k):
        side = (zb + k) % 2
        arrivals = (1, 4, 3, 0, 5) if k == 0 else range(7)
        for n in arrivals:
            p_arrival(k, n).wait_recv()
        acc = psend[side, yl, x].astype(F32)
        for n in arrivals:
            sx, sy = plane_src(*plane[n])
            acc = acc + precv[side, sy, sx].astype(F32)
        rsum[side] = acc.astype(BF16).reshape(2, 128, 128)
        for u in range(2):

            @pl.when(jnp.logical_not(hid_source_is_me(side, u)))
            def _():
                q_copy(k, u).start()

            @pl.when(hid_source_is_me(side, u))
            def _():
                own = pltpu.make_async_copy(rsum.at[side, u], qrecv.at[yh % 2, c], lsem)
                own.start()
                own.wait()

    def g_relays(part):
        half = slice(part * 64, part * 64 + 64)
        for j in range(2):
            g_relay(j, part).wait_recv()
            to = (za + (1, 3)[j]) % 4
            own = gsend[to, j, half].astype(F32)
            gsend[to, j, half] = (own + grelay[j, half].astype(F32)).astype(BF16)
            g_on(j, part).start()

    g_relays(0)
    for n in range(7):
        dot_copy(n).wait_recv()
    value = dots[seq(zb, yh)]
    for n in range(7):
        value = value + dots_in[n]
    sums[2] = value
    for n in range(15):
        mean_copy(n).start()
    g_relays(1)

    owners(0)
    owners(1)

    g_sibling().wait_recv()
    for h in range(2):
        g_arrival(h).wait_recv()
        for part in range(2):
            g_on_arrival(h, part).wait_recv()
    grecv[za, c] = gsend[za, c]
    for h in range(2):
        acc = grecv[za, h].astype(F32)
        for d in range(2):
            acc = acc + grecv[(za + (3, 1)[d]) % 4, h].astype(F32)
        wgrad_ref[h * 128 : (h + 1) * 128, :] = acc.astype(BF16)

    wgrad_out = pltpu.make_async_copy(wgrad_ref, wgrad_hbm, isem.at[7])
    wgrad_out.start()
    dot = sums[2]
    for n in range(15):
        mean_copy(n).wait_recv()
        dot = dot + sums_in[1, n]
    factor = column_of(dot * (1.0 / 8192.0) / mean_square)
    inv_column = column_of(inv_root)
    for i in range(2):
        for h in range(2):

            @pl.when(jnp.logical_not(hid_target_is_me(i, h)))
            def _():
                remote(rsum.at[0, 0], qrecv.at[i, h], S_Q + 2 * i + h, sibling).wait_recv()

    for i in range(2):
        for h in range(2):
            k = 2 * i + h
            part = slice(k * 128, (k + 1) * 128)
            grad = qrecv[i, h].astype(F32) * gain[:, part]
            igrad_ref[:, part] = ((grad - hid[:, part] * factor) * inv_column).astype(BF16)

    igrad_out = pltpu.make_async_copy(igrad_ref, igrad_hbm, isem.at[8])
    igrad_out.start()

    for i in range(2):
        for h in range(2):

            @pl.when(jnp.logical_not(hid_target_is_me(i, h)))
            def _():
                hid_copy(i, h).wait_send()

    for k in range(2):
        for u in range(2):

            @pl.when(jnp.logical_not(hid_source_is_me((zb + k) % 2, u)))
            def _():
                q_copy(k, u).wait_send()

    sq_sibling.wait_send()
    for n in range(7):
        sq_copy(n).wait_send()
    for n in range(15):
        mean_copy(n).wait_send()
    gram_copy.wait_send()
    for n in range(5):
        w_copy(n).wait_send()
    g_sibling().wait_send()
    for j in range(2):
        w_on(j).wait_send()
        g_copy(j).wait_send()
        for part in range(2):
            g_relay(j, part).wait_send()
            g_on(j, part).wait_send()
    for n in range(7):
        for k in range(2):
            if n % 4 != 2:
                h_copy(k, n).wait_send()
            else:
                hid_far(k, n // 4).wait_send()
        if n % 4 != 2:
            p_copy(0, n).wait_send()
        else:
            p_far(n // 4).wait_send()
        p_copy(1, n).wait_send()
        inv_copy(n).wait_send()
        dot_copy(n).wait_send()
    for dy in range(4):
        if dy % 2:
            d_y(dy).wait_send()
            d_far(dy).wait_send()
        d_z(dy).wait_send()
        d_c(0, dy).wait_send()
        d_c(1, dy).wait_send()
    wgrad_out.wait()
    igrad_out.wait()


def hand_over(igrad_ref, wgrad_ref, igrad_out, wgrad_out, igrad, wgrad, sem):
    ins = [
        pltpu.make_async_copy(igrad_ref, igrad, sem.at[0]),
        pltpu.make_async_copy(wgrad_ref, wgrad, sem.at[1]),
    ]
    outs = [
        pltpu.make_async_copy(igrad, igrad_out, sem.at[2]),
        pltpu.make_async_copy(wgrad, wgrad_out, sem.at[3]),
    ]
    for copy in ins:
        copy.start()
    for first, second in zip(ins, outs):
        first.wait()
        second.start()
    for copy in outs:
        copy.wait()


def shards(hidden, gain, proj_weight, b_c, ssm_x, dy, log_decay):
    hbm = pl.BlockSpec(memory_space=pl.ANY)
    grads = pl.pallas_call(
        kernel,
        out_shape=(
            jax.ShapeDtypeStruct(hidden.shape, BF16),
            jax.ShapeDtypeStruct(proj_weight.shape, BF16),
        ),
        in_specs=[hbm] * 7,
        out_specs=(hbm, hbm),
        scratch_shapes=[
            pltpu.VMEM(hidden.shape, BF16),
            pltpu.VMEM(proj_weight.shape, BF16),
            pltpu.VMEM(hidden.shape, BF16),
            pltpu.VMEM(gain.shape, BF16),
            pltpu.VMEM(proj_weight.shape, BF16),
            pltpu.VMEM(b_c.shape, BF16),
            pltpu.VMEM(ssm_x.shape, BF16),
            pltpu.VMEM(dy.shape, BF16),
            pltpu.VMEM(log_decay.shape[::-1], F32),
            pltpu.VMEM((4, 128, 128), BF16),
            pltpu.VMEM((2, 4, 128, 512), BF16),
            pltpu.VMEM((2, 4, 128, 512), BF16),
            pltpu.VMEM((2, 4, 128, 256), BF16),
            pltpu.VMEM((3, 1, 128), F32),
            pltpu.VMEM((2, 15, 1, 128), F32),
            pltpu.VMEM((2, 2, 2, 1, 128), F32),
            pltpu.VMEM((2, 2, 2, 1, 128), F32),
            pltpu.VMEM((7, 1, 128), F32),
            pltpu.VMEM((2, 128, 128), F32),
            pltpu.VMEM((2, 2, 2, 2, 128, 256), BF16),
            pltpu.VMEM((2, 2, 4, 256, 128), BF16),
            pltpu.VMEM((2, 2, 4, 256, 128), BF16),
            pltpu.VMEM((2, 2, 128, 128), BF16),
            pltpu.VMEM((2, 2, 128, 128), BF16),
            pltpu.VMEM((4, 2, 128, 256), BF16),
            pltpu.VMEM((4, 2, 128, 256), BF16),
            pltpu.VMEM((2, 128, 256), BF16),
            pltpu.VMEM((2, 256, 128), BF16),
            pltpu.SemaphoreType.DMA((N_SLOTS,)),
            pltpu.SemaphoreType.DMA((N_SLOTS,)),
            pltpu.SemaphoreType.DMA,
            pltpu.SemaphoreType.DMA((9,)),
        ],
        compiler_params=pltpu.CompilerParams(
            collective_id=0, has_side_effects=True, vmem_limit_bytes=63 * 1024 * 1024
        ),
        name="projection_backward",
    )(hidden, gain, proj_weight, b_c, ssm_x, dy, log_decay.T)
    return pl.pallas_call(
        hand_over,
        out_shape=tuple(jax.ShapeDtypeStruct(grad.shape, grad.dtype) for grad in grads),
        in_specs=[hbm] * 2,
        out_specs=(hbm, hbm),
        scratch_shapes=[
            pltpu.VMEM(hidden.shape, BF16),
            pltpu.VMEM(proj_weight.shape, BF16),
            pltpu.SemaphoreType.DMA((4,)),
        ],
        compiler_params=pltpu.CompilerParams(vmem_limit_bytes=63 * 1024 * 1024),
        name="hand_over",
    )(*grads)


def solution(mesh):
    return jax.shard_map(
        shards,
        mesh=mesh,
        in_specs=(
            P("dp", "tensor"),
            P("tensor"),
            P("dp", "tensor"),
            P("dp", "tensor"),
            P("dp", "tensor"),
            P("dp", "tensor"),
            P("dp", "tensor"),
        ),
        out_specs=(P("dp", "tensor"), P("dp", "tensor")),
        check_vma=False,
    )
```

```python
import jax
import jax.numpy as jnp
from jax import lax
from jax.experimental import pallas as pl
from jax.experimental.pallas import tpu as pltpu
from jax.sharding import PartitionSpec as P

MHEAD = 64
EPSILON = 1e-05
MESH = pl.DeviceIdType.MESH
F32 = jnp.float32
BF16 = jnp.bfloat16
HIGHEST = lax.Precision.HIGHEST


def device(za, zb, yh, x, yl, c):
    return {"dp": (za * 2 + zb) * 4 + yh, "tensor": x * 4 + yl * 2 + c}


def nt_dot(a, b, precision=None):
    return lax.dot_general(
        a, b, (((1,), (1,)), ((), ())), preferred_element_type=F32, precision=precision
    )


def nn_dot(a, b, precision=None):
    return lax.dot_general(
        a, b, (((1,), (0,)), ((), ())), preferred_element_type=F32, precision=precision
    )


class Slots:
    def __init__(self):
        self.count = 0

    def take(self, n):
        first = self.count
        self.count += n
        return first


SLOTS = Slots()
S_HID = SLOTS.take(4)
S_HAG = SLOTS.take(14)
S_W = SLOTS.take(7)
S_SQ = SLOTS.take(8)
S_INV = SLOTS.take(8)
S_GRAM = SLOTS.take(1)
S_DY = SLOTS.take(4)
S_DZ = SLOTS.take(4)
S_DC = SLOTS.take(8)
S_P = SLOTS.take(14)
S_Q = SLOTS.take(4)
S_G = SLOTS.take(3)
S_GIN = SLOTS.take(4)
S_GON = SLOTS.take(4)
S_DOT = SLOTS.take(8)
S_MEAN = SLOTS.take(15)
N_SLOTS = SLOTS.count


def kernel(
    hid_hbm,
    gain_hbm,
    w_hbm,
    bc_hbm,
    x_hbm,
    dy_hbm,
    ld_hbm,
    igrad_hbm,
    wgrad_hbm,
    igrad_ref,
    wgrad_ref,
    hid_ref,
    gain_ref,
    w_ref,
    bc_ref,
    x_ref,
    dy_ref,
    ld_ref,
    ht,
    hall,
    hscaled,
    wall,
    sums,
    sums_in,
    inv,
    dots,
    dots_in,
    gram,
    dall,
    psend,
    precv,
    rsum,
    qrecv,
    gsend,
    grecv,
    grelay,
    prelay,
    ssem,
    rsem,
    lsem,
    isem,
):
    loads = [
        pltpu.make_async_copy(src, dst, isem.at[n])
        for n, (src, dst) in enumerate(
            (
                (hid_hbm, hid_ref),
                (gain_hbm, gain_ref),
                (w_hbm, w_ref),
                (ld_hbm, ld_ref),
                (x_hbm, x_ref),
                (dy_hbm, dy_ref),
                (bc_hbm, bc_ref),
            )
        )
    ]
    for load in loads:
        load.start()

    dp = lax.axis_index("dp")
    ten = lax.axis_index("tensor")
    z, yh = dp // 4, dp % 4
    za, zb = z // 2, z % 2
    x, yl, c = ten // 4, (ten // 2) % 2, ten % 2

    def remote(src, dst, slot, dev, rslot=None):
        rslot = slot if rslot is None else rslot
        return pltpu.make_async_remote_copy(
            src_ref=src,
            dst_ref=dst,
            send_sem=ssem.at[slot],
            recv_sem=rsem.at[rslot],
            device_id=device(*dev),
            device_id_type=MESH,
        )

    sibling = (za, zb, yh, x, yl, 1 - c)
    plane = [(1, 0), (3, 0), (2, 0), (0, 1), (1, 1), (3, 1), (2, 1)]
    column = [(0, 1), (0, 3), (0, 2), (1, 0), (1, 1), (1, 3), (1, 2)]
    depth = [(dza, fc) for dza in (1, 3) for fc in range(2)] + [(0, 1)]
    tensor = [(0, 0, 1)] + [(dx, fy, fc) for fc in range(2) for dx, fy in plane]

    def plane_dev(dx, fy):
        return (za, zb, yh, (x + dx) % 4, (yl + fy) % 2, c)

    def plane_src(dx, fy):
        return (x + 4 - dx) % 4, (yl + fy) % 2

    def tensor_dev(dx, fy, fc):
        return (za, zb, yh, (x + dx) % 4, (yl + fy) % 2, (c + fc) % 2)

    def column_dev(k, dy):
        return (za, (zb + k) % 2, (yh + dy) % 4, x, yl, c)

    def far(dza, fc):
        return ((za + dza) % 4, zb, yh, x, yl, (c + fc) % 2)

    def seq(side, y):
        return (y % 2, side, y // 2)

    def hid_target(i, h):
        return (za, yl, 2 * c + i, x, yh % 2, h)

    def hid_target_is_me(i, h):
        return (yl == zb) & (yh == 2 * c + i) & (yl == yh % 2) & (c == h)

    def hid_source(side, u):
        return (za, side, yl + 2 * u, x, zb, yh // 2)

    def hid_source_is_me(side, u):
        return (side == zb) & (yl + 2 * u == yh) & (yl == zb) & (c == yh // 2)

    barrier = pltpu.get_barrier_semaphore()

    def greet(dev):
        pl.semaphore_signal(barrier, inc=1, device_id=device(*dev), device_id_type=MESH)

    for dx, fy, fc in tensor:
        greet(tensor_dev(dx, fy, fc))
    for k, dy in column:
        greet(column_dev(k, dy))
    for dza, fc in depth[:-1]:
        greet(far(dza, fc))
    met = 15 + 7 + 4
    for i in range(2):
        for h in range(2):

            @pl.when(jnp.logical_not(hid_target_is_me(i, h)))
            def _():
                greet(hid_target(i, h))

    for side in range(2):
        for u in range(2):

            @pl.when(jnp.logical_not(hid_source_is_me(side, u)))
            def _():
                greet(hid_source(side, u))

    own_hop = jnp.where((yl == zb) & (yl == yh % 2) & (c == yh // 2), 1, 0)

    for load in loads[:3]:
        load.wait()
    hid = hid_ref[...].astype(F32)
    gain = gain_ref[...].astype(F32).reshape(1, -1)
    scaled = hid * gain
    for k in range(4):
        ht[k] = scaled[:, k * 128 : (k + 1) * 128].T.astype(BF16)

    def row_of(column):
        return jnp.broadcast_to(column, (128, 128)).T[0:1, :]

    def column_of(row):
        return jnp.broadcast_to(row[0:1, :], (128, 128)).T

    sums[0] = row_of(jnp.sum(hid * hid, axis=1, keepdims=True))
    wall[c, za] = w_ref[pl.ds(pl.multiple_of(c * 128, 128), 128), :]

    pl.semaphore_wait(barrier, met + 8 - 2 * own_hop)

    sq_sibling = remote(sums.at[0], sums_in.at[0, 0], S_SQ, sibling)
    sq_sibling.start()

    def sq_copy(n):
        return remote(sums.at[1], sums_in.at[0, 1 + n], S_SQ + 1 + n, plane_dev(*plane[n]))

    def mean_copy(n):
        return remote(sums.at[2], sums_in.at[1, n], S_MEAN + n, tensor_dev(*tensor[n]))

    def hid_copy(i, h):
        lane = (2 * zb + yh // 2) * 128
        return remote(
            ht.at[2 * i + h],
            hall.at[yh % 2, x, :, pl.ds(pl.multiple_of(lane, 128), 128)],
            S_HID + 2 * i + h,
            hid_target(i, h),
            S_HID + 2 * zb + yh // 2,
        )

    def hid_arrival(side, u):
        lane = (2 * side + u) * 128
        return remote(
            ht.at[0],
            hall.at[yl, x, :, pl.ds(pl.multiple_of(lane, 128), 128)],
            S_HID + 2 * side + u,
            sibling,
        )

    for i in range(2):
        for h in range(2):

            @pl.when(jnp.logical_not(hid_target_is_me(i, h)))
            def _():
                hid_copy(i, h).start()

            @pl.when(hid_target_is_me(i, h))
            def _():
                lane = (2 * zb + yh // 2) * 128
                own = pltpu.make_async_copy(
                    ht.at[2 * i + h],
                    hall.at[yl, x, :, pl.ds(pl.multiple_of(lane, 128), 128)],
                    lsem,
                )
                own.start()
                own.wait()

    def w_copy(n):
        dza, fc = depth[n]
        core = (c + fc) % 2
        return remote(
            w_ref.at[pl.ds(pl.multiple_of(core * 128, 128), 128), :],
            wall.at[c, za],
            S_W + n,
            far(dza, fc),
        )

    def w_arrival(n):
        dza, fc = depth[n]
        return remote(
            w_ref.at[0:128, :], wall.at[(c + fc) % 2, (za + 4 - dza) % 4], S_W + n, sibling
        )

    for n in range(5):
        w_copy(n).start()

    def w_on(j):
        block = wall.at[j, (za + (1, 3)[j] + 2) % 4]
        return remote(block, block, S_W + 5 + j, far((1, 3)[j], 0))

    def w_on_arrival(j):
        block = wall.at[j, (za + 2) % 4]
        return remote(block, block, S_W + 5 + j, sibling)

    for load in loads[3:]:
        load.wait()
    rows = lax.broadcasted_iota(jnp.int32, (128, 128), 0)
    cols = lax.broadcasted_iota(jnp.int32, (128, 128), 1)
    causal = rows >= cols
    heads = ld_ref.shape[0]
    padded = jnp.concatenate([ld_ref[...], jnp.zeros((128 - heads, 128), F32)], axis=0)
    running_t = nt_dot(padded, causal.astype(F32), HIGHEST)
    running = running_t.T
    low = cols < MHEAD
    total = jnp.zeros((128, 128), F32)
    for p in range(heads // 2):
        xp = x_ref[:, p * 128 : (p + 1) * 128]
        zero = jnp.zeros_like(xp)
        both = jnp.concatenate([jnp.where(low, xp, zero), jnp.where(low, zero, xp)], axis=0)
        inner = nt_dot(dy_ref[:, p * 128 : (p + 1) * 128], both)
        for k in range(2):
            h = 2 * p + k
            gap = running[:, h : h + 1] - running_t[h : h + 1, :]
            decay = jnp.exp(jnp.where(causal, gap, -1e30))
            total = total + inner[:, k * 128 : (k + 1) * 128] * decay
    gram[0] = total

    gram_copy = remote(gram.at[0], gram.at[1], S_GRAM, sibling)
    gram_copy.start()

    sq_sibling.wait_recv()
    sums[1] = sums[0] + sums_in[0, 0]
    for n in range(7):
        sq_copy(n).start()

    gram_copy.wait_recv()
    total = gram[0] + gram[1]
    bc = bc_ref[...].astype(F32)
    grad_b = nn_dot(total.T, bc[:, 128:], HIGHEST)
    grad_c = nn_dot(total, bc[:, :128], HIGHEST)
    dall[(c,) + seq(zb, yh)] = jnp.concatenate([grad_b, grad_c], axis=1).astype(BF16)

    def d_y(dy):
        block = dall.at[(c,) + seq(zb, yh)]
        return remote(block, block, S_DY + dy, column_dev(0, dy))

    def d_far(dy):
        half = slice(0, 64) if dy == 1 else slice(64, 128)
        block = dall.at[(c,) + seq(zb, (yh + 4 - dy) % 4) + (half,)]
        return remote(block, block, S_DY + dy - 1, column_dev(0, dy))

    def d_far_arrival(dy):
        half = slice(0, 64) if dy == 1 else slice(64, 128)
        block = dall.at[(c,) + seq(zb, (yh + 2) % 4) + (half,)]
        return remote(block, block, S_DY + dy - 1, sibling)

    def d_y_arrival(dy):
        block = dall.at[(c,) + seq(zb, (yh + 4 - dy) % 4)]
        return remote(block, block, S_DY + dy, sibling)

    def d_z(dy):
        if dy == 2:
            block = dall.at[(c,) + seq(1 - zb, yh)]
            return remote(block, block, S_DZ + dy, column_dev(0, 2))
        block = dall.at[(c,) + seq(zb, (yh + 4 - dy) % 4)]
        return remote(block, block, S_DZ + dy, column_dev(1, 0))

    def d_z_arrival(dy):
        block = dall.at[(c,) + seq(1 - zb, (yh + 4 - dy) % 4)]
        return remote(block, block, S_DZ + dy, sibling)

    def d_c(k, dy):
        block = dall.at[(c,) + seq((zb + k) % 2, (yh + 4 - dy) % 4)]
        return remote(block, block, S_DC + 4 * k + dy, sibling)

    def d_c_arrival(k, dy):
        block = dall.at[(1 - c,) + seq((zb + k) % 2, (yh + 4 - dy) % 4)]
        return remote(block, block, S_DC + 4 * k + dy, sibling)

    for dy in (1, 3):
        d_y(dy).start()
    d_z(0).start()
    d_c(0, 0).start()

    def h_block(k, sy, sx):
        lane = ((zb + k) % 2) * 256
        return hall.at[sy, sx, :, pl.ds(pl.multiple_of(lane, 128), 256)]

    def h_copy(k, n):
        dx, fy = plane[n]
        block = h_block(k, (yl + fy) % 2 if dx else yl, x)
        dev = (za, zb, yh, (x + dx) % 4, yl if dx else 1 - yl, c)
        return remote(block, block, S_HAG + 7 * k + n, dev)

    def h_arrival(k, n):
        sx, sy = plane_src(*plane[n])
        block = h_block(k, sy, sx)
        return remote(block, block, S_HAG + 7 * k + n, sibling)

    def hid_on(k):
        side = (zb + k) % 2
        for u in range(2):

            @pl.when(jnp.logical_not(hid_source_is_me(side, u)))
            def _():
                hid_arrival(side, u).wait_recv()

        for n in (3, 0, 1):
            h_copy(k, n).start()

    def hid_across(k):
        h_arrival(k, 3).wait_recv()
        for n in (4, 5):
            h_copy(k, n).start()

    def hid_far(k, fy):
        sx, sy = plane_src((1, 3)[k], fy)
        block = h_block(k, sy, sx)
        slot = S_HAG + 7 * k + 2 + 4 * fy
        return remote(block, block, slot, (za, zb, yh, (x + (1, 3)[k]) % 4, yl, c))

    def hid_relay(k, fy):
        h_arrival(k, k + 4 * fy).wait_recv()
        hid_far(k, fy).start()

    hid_on(0)
    hid_on(1)

    def d_on(dy):
        if dy == 2:
            d_far_arrival(1).wait_recv()
            d_far_arrival(3).wait_recv()
        else:
            d_y_arrival(dy).wait_recv()
            d_far(dy).start()
            d_z(dy).start()
        d_c(0, dy).start()

    square = sums[1]
    for n in range(7):
        sq_copy(n).wait_recv()
        square = square + sums_in[0, 1 + n]
    mean_square = square * (1.0 / 8192.0) + EPSILON
    inv_root = lax.rsqrt(mean_square)
    inv[seq(zb, yh)] = inv_root

    def inv_copy(n):
        block = inv.at[seq(zb, yh)]
        return remote(block, block, S_INV + n, column_dev(*column[n]))

    def inv_arrival(n):
        k, dy = column[n]
        block = inv.at[seq((zb + k) % 2, (yh + 4 - dy) % 4)]
        return remote(block, block, S_INV + n, sibling)

    for n in range(7):
        inv_copy(n).start()

    d_on(1)
    d_on(3)
    for n in range(4):
        w_arrival(n).wait_recv()
    for j in range(2):
        w_on(j).start()
    d_z_arrival(0).wait_recv()
    d_z(2).start()
    d_c(1, 0).start()
    hid_across(0)
    hid_relay(0, 0)
    hid_relay(1, 0)
    hid_across(1)

    d_on(2)
    for dy in (0, 1, 3, 2):
        d_c_arrival(0, dy).wait_recv()

    def p_copy(k, n):
        dx, fy = plane[n]
        side = (zb + k) % 2
        relayed = k == 0 and (dx, fy) in ((1, 0), (3, 1))
        return remote(
            prelay.at[fy] if relayed else psend.at[side, (yl + fy) % 2, (x + dx) % 4],
            precv.at[side, yl, x],
            S_P + 7 * k + n,
            plane_dev(dx, fy),
        )

    def p_arrival(k, n):
        sx, sy = plane_src(*plane[n])
        block = precv.at[(zb + k) % 2, sy, sx]
        return remote(block, block, S_P + 7 * k + n, sibling)

    def terms(k, dza):
        side, tx = (zb + k) % 2, (za + dza) % 4
        for py in range(2):
            out = nt_dot(dall[0, py, side].reshape(256, 256), wall[0, tx])
            out = out + nt_dot(dall[1, py, side].reshape(256, 256), wall[1, tx])
            psend[side, py, tx] = out.astype(BF16)

    def p_far(fy):
        block = psend.at[zb, (yl + fy) % 2, (x + 2) % 4]
        dev = (za, zb, yh, (x + (1, 3)[fy]) % 4, yl, c)
        return remote(block, prelay.at[fy], S_P + 2 + 4 * fy, dev)

    def p_relay(fy):
        p_far(fy).wait_recv()
        to = (yl + fy) % 2, (x + (1, 3)[fy]) % 4
        own = psend[(zb,) + to].astype(F32)
        prelay[fy] = (own + prelay[fy].astype(F32)).astype(BF16)
        p_copy(0, 5 * fy).start()

    def p_start(k, dza):
        for n, (dx, fy) in enumerate(plane):
            if (dx, fy) in ((1, 0), (3, 1)):
                continue

            @pl.when((x + dx) % 4 == (za + dza) % 4)
            def _():
                if dx == 2:
                    p_far(fy).start()
                else:
                    p_copy(k, n).start()

    w_arrival(4).wait_recv()
    for dza in (0, 1, 3):
        terms(0, dza)
    hid_relay(0, 1)
    hid_relay(1, 1)
    for dza in (0, 1, 3):
        p_start(0, dza)
    for j in range(2):
        w_on_arrival(j).wait_recv()
    terms(0, 2)
    p_start(0, 2)
    for dy in (1, 3, 2):
        d_z_arrival(dy).wait_recv()
        d_c(1, dy).start()
    for dy in (0, 1, 3, 2):
        d_c_arrival(1, dy).wait_recv()
    for dza in range(4):
        terms(1, dza)

    def g_dev(dza, j):
        return ((za + dza) % 4, zb, yh, x, yl, j)

    def g_copy(j):
        dza = (3, 1)[j]
        return remote(
            gsend.at[(za + dza) % 4, j], grecv.at[za, c], S_G + j, g_dev(dza, j), S_G + c
        )

    def g_arrival(h):
        block = grecv.at[jnp.where(c == 0, (za + 1) % 4, (za + 3) % 4), h]
        return remote(block, block, S_G + h, sibling)

    def g_sibling():
        return remote(gsend.at[za, 1 - c], grecv.at[za, c], S_G + 2, sibling)

    def g_relay(j, part):
        half = slice(part * 64, part * 64 + 64)
        return remote(
            gsend.at[(za + 2) % 4, j, half],
            grelay.at[j, half],
            S_GIN + 2 * j + part,
            g_dev((1, 3)[j], c),
        )

    def g_on(j, part):
        dza = (1, 3)[j]
        half = slice(part * 64, part * 64 + 64)
        return remote(
            gsend.at[(za + dza) % 4, j, half],
            grecv.at[za, c, half],
            S_GON + 2 * j + part,
            g_dev(dza, j),
            S_GON + 2 * c + part,
        )

    def g_on_arrival(h, part):
        half = slice(part * 64, part * 64 + 64)
        block = grecv.at[jnp.where(c == 0, (za + 3) % 4, (za + 1) % 4), h, half]
        return remote(block, block, S_GON + 2 * h + part, sibling)

    for n in range(7):
        inv_arrival(n).wait_recv()
    inv_rows = [
        jnp.concatenate([inv[sy, side, u][0:1, :] for side in range(2) for u in range(2)], axis=1)
        for sy in range(2)
    ]
    inv_rows = [inv_rows[sy] * (1.0 / 64.0) for sy in range(2)]
    own_inv = jnp.where(yl == 0, inv_rows[0], inv_rows[1])
    other_inv = jnp.where(yl == 0, inv_rows[1], inv_rows[0])

    def scale(dx, fy):
        sx, sy = plane_src(dx, fy)
        row = other_inv if fy else own_inv
        hscaled[sy, sx] = (hall[sy, sx].astype(F32) * row).astype(BF16)

    scale(0, 0)
    scale(0, 1)
    for n in (0, 1, 4, 5, 2, 6):
        for k in range(2):
            if n % 4 != k:
                h_arrival(k, n).wait_recv()
        scale(*plane[n])
    eye = (rows == cols).astype(F32)
    for py in range(2):
        for side in range(2):
            for u in range(2):
                part = slice(u * 128, (u + 1) * 128)
                lane = (2 * side + u) * 128
                prod = jnp.zeros((128, 128), F32)
                for f in range(4):
                    prod = prod + nn_dot(
                        psend[side, py, f, part, :], hall[py, f, :, lane : lane + 128]
                    )
                row = jnp.sum(prod * eye, axis=0, keepdims=True)
                dots[py, side, u] = row

    def dot_copy(n):
        k, dy = column[n]
        block = dots.at[seq((zb + k) % 2, (yh + dy) % 4)]
        return remote(block, dots_in.at[n], S_DOT + n, column_dev(k, dy))

    for n in range(7):
        dot_copy(n).start()
    p_relay(0)
    p_relay(1)
    for n in range(7):
        p_copy(1, n).start()

    def g_terms(first, count, j):
        rows = [hscaled[sy, pl.ds(first, count)].reshape(count * 128, 512) for sy in range(2)]
        out = nn_dot(rows[0], dall[j, 0].reshape(512, 256))
        out = out + nn_dot(rows[1], dall[j, 1].reshape(512, 256))
        gsend[pl.ds(first, count), j] = out.astype(BF16).reshape(count, 128, 256)

    for j in range(2):
        g_terms((za + 2) % 4, 1, j)
        g_relay(j, 0).start()
    for j in range(2):
        g_relay(j, 1).start()
    for j in range(2):
        g_terms((za + (3, 1)[j]) % 4, 1, j)
        g_copy(j).start()
    for j in range(2):
        g_terms((za + (1, 3)[j]) % 4, 1, j)
        g_terms(za, 1, j)
    g_sibling().start()

    def q_copy(k, u):
        side = (zb + k) % 2
        return remote(
            rsum.at[side, u],
            qrecv.at[yh % 2, c],
            S_Q + 2 * k + u,
            hid_source(side, u),
            S_Q + 2 * (yh % 2) + c,
        )

    def owners(k):
        side = (zb + k) % 2
        arrivals = (1, 4, 3, 0, 5) if k == 0 else range(7)
        for n in arrivals:
            p_arrival(k, n).wait_recv()
        acc = psend[side, yl, x].astype(F32)
        for n in arrivals:
            sx, sy = plane_src(*plane[n])
            acc = acc + precv[side, sy, sx].astype(F32)
        rsum[side] = acc.astype(BF16).reshape(2, 128, 128)
        for u in range(2):

            @pl.when(jnp.logical_not(hid_source_is_me(side, u)))
            def _():
                q_copy(k, u).start()

            @pl.when(hid_source_is_me(side, u))
            def _():
                own = pltpu.make_async_copy(rsum.at[side, u], qrecv.at[yh % 2, c], lsem)
                own.start()
                own.wait()

    def g_relays(part):
        half = slice(part * 64, part * 64 + 64)
        for j in range(2):
            g_relay(j, part).wait_recv()
            to = (za + (1, 3)[j]) % 4
            own = gsend[to, j, half].astype(F32)
            gsend[to, j, half] = (own + grelay[j, half].astype(F32)).astype(BF16)
            g_on(j, part).start()

    g_relays(0)
    for n in range(7):
        dot_copy(n).wait_recv()
    value = dots[seq(zb, yh)]
    for n in range(7):
        value = value + dots_in[n]
    sums[2] = value
    for n in range(15):
        mean_copy(n).start()
    g_relays(1)

    owners(0)
    owners(1)

    g_sibling().wait_recv()
    for h in range(2):
        g_arrival(h).wait_recv()
        for part in range(2):
            g_on_arrival(h, part).wait_recv()
    grecv[za, c] = gsend[za, c]
    for h in range(2):
        acc = grecv[za, h].astype(F32)
        for d in range(2):
            acc = acc + grecv[(za + (3, 1)[d]) % 4, h].astype(F32)
        wgrad_ref[h * 128 : (h + 1) * 128, :] = acc.astype(BF16)

    wgrad_out = pltpu.make_async_copy(wgrad_ref, wgrad_hbm, isem.at[7])
    wgrad_out.start()
    dot = sums[2]
    for n in range(15):
        mean_copy(n).wait_recv()
        dot = dot + sums_in[1, n]
    factor = column_of(dot * (1.0 / 8192.0) / mean_square)
    inv_column = column_of(inv_root)
    for i in range(2):
        for h in range(2):

            @pl.when(jnp.logical_not(hid_target_is_me(i, h)))
            def _():
                remote(rsum.at[0, 0], qrecv.at[i, h], S_Q + 2 * i + h, sibling).wait_recv()

    for i in range(2):
        for h in range(2):
            k = 2 * i + h
            part = slice(k * 128, (k + 1) * 128)
            grad = qrecv[i, h].astype(F32) * gain[:, part]
            igrad_ref[:, part] = ((grad - hid[:, part] * factor) * inv_column).astype(BF16)

    igrad_out = pltpu.make_async_copy(igrad_ref, igrad_hbm, isem.at[8])
    igrad_out.start()

    for i in range(2):
        for h in range(2):

            @pl.when(jnp.logical_not(hid_target_is_me(i, h)))
            def _():
                hid_copy(i, h).wait_send()

    for k in range(2):
        for u in range(2):

            @pl.when(jnp.logical_not(hid_source_is_me((zb + k) % 2, u)))
            def _():
                q_copy(k, u).wait_send()

    sq_sibling.wait_send()
    for n in range(7):
        sq_copy(n).wait_send()
    for n in range(15):
        mean_copy(n).wait_send()
    gram_copy.wait_send()
    for n in range(5):
        w_copy(n).wait_send()
    g_sibling().wait_send()
    for j in range(2):
        w_on(j).wait_send()
        g_copy(j).wait_send()
        for part in range(2):
            g_relay(j, part).wait_send()
            g_on(j, part).wait_send()
    for n in range(7):
        for k in range(2):
            if n % 4 != 2:
                h_copy(k, n).wait_send()
            else:
                hid_far(k, n // 4).wait_send()
        if n % 4 != 2:
            p_copy(0, n).wait_send()
        else:
            p_far(n // 4).wait_send()
        p_copy(1, n).wait_send()
        inv_copy(n).wait_send()
        dot_copy(n).wait_send()
    for dy in range(4):
        if dy % 2:
            d_y(dy).wait_send()
            d_far(dy).wait_send()
        d_z(dy).wait_send()
        d_c(0, dy).wait_send()
        d_c(1, dy).wait_send()
    wgrad_out.wait()
    igrad_out.wait()


def hand_over(igrad_ref, wgrad_ref, igrad_out, wgrad_out, igrad, wgrad, sem):
    ins = [
        pltpu.make_async_copy(igrad_ref, igrad, sem.at[0]),
        pltpu.make_async_copy(wgrad_ref, wgrad, sem.at[1]),
    ]
    outs = [
        pltpu.make_async_copy(igrad, igrad_out, sem.at[2]),
        pltpu.make_async_copy(wgrad, wgrad_out, sem.at[3]),
    ]
    for copy in ins:
        copy.start()
    for first, second in zip(ins, outs):
        first.wait()
        second.start()
    for copy in outs:
        copy.wait()


def shards(hidden, gain, proj_weight, b_c, ssm_x, dy, log_decay):
    hbm = pl.BlockSpec(memory_space=pl.ANY)
    grads = pl.pallas_call(
        kernel,
        out_shape=(
            jax.ShapeDtypeStruct(hidden.shape, BF16),
            jax.ShapeDtypeStruct(proj_weight.shape, BF16),
        ),
        in_specs=[hbm] * 7,
        out_specs=(hbm, hbm),
        scratch_shapes=[
            pltpu.VMEM(hidden.shape, BF16),
            pltpu.VMEM(proj_weight.shape, BF16),
            pltpu.VMEM(hidden.shape, BF16),
            pltpu.VMEM(gain.shape, BF16),
            pltpu.VMEM(proj_weight.shape, BF16),
            pltpu.VMEM(b_c.shape, BF16),
            pltpu.VMEM(ssm_x.shape, BF16),
            pltpu.VMEM(dy.shape, BF16),
            pltpu.VMEM(log_decay.shape[::-1], F32),
            pltpu.VMEM((4, 128, 128), BF16),
            pltpu.VMEM((2, 4, 128, 512), BF16),
            pltpu.VMEM((2, 4, 128, 512), BF16),
            pltpu.VMEM((2, 4, 128, 256), BF16),
            pltpu.VMEM((3, 1, 128), F32),
            pltpu.VMEM((2, 15, 1, 128), F32),
            pltpu.VMEM((2, 2, 2, 1, 128), F32),
            pltpu.VMEM((2, 2, 2, 1, 128), F32),
            pltpu.VMEM((7, 1, 128), F32),
            pltpu.VMEM((2, 128, 128), F32),
            pltpu.VMEM((2, 2, 2, 2, 128, 256), BF16),
            pltpu.VMEM((2, 2, 4, 256, 128), BF16),
            pltpu.VMEM((2, 2, 4, 256, 128), BF16),
            pltpu.VMEM((2, 2, 128, 128), BF16),
            pltpu.VMEM((2, 2, 128, 128), BF16),
            pltpu.VMEM((4, 2, 128, 256), BF16),
            pltpu.VMEM((4, 2, 128, 256), BF16),
            pltpu.VMEM((2, 128, 256), BF16),
            pltpu.VMEM((2, 256, 128), BF16),
            pltpu.SemaphoreType.DMA((N_SLOTS,)),
            pltpu.SemaphoreType.DMA((N_SLOTS,)),
            pltpu.SemaphoreType.DMA,
            pltpu.SemaphoreType.DMA((9,)),
        ],
        compiler_params=pltpu.CompilerParams(
            collective_id=0, has_side_effects=True, vmem_limit_bytes=63 * 1024 * 1024
        ),
        name="projection_backward",
    )(hidden, gain, proj_weight, b_c, ssm_x, dy, log_decay.T)
    return pl.pallas_call(
        hand_over,
        out_shape=tuple(jax.ShapeDtypeStruct(grad.shape, grad.dtype) for grad in grads),
        in_specs=[hbm] * 2,
        out_specs=(hbm, hbm),
        scratch_shapes=[
            pltpu.VMEM(hidden.shape, BF16),
            pltpu.VMEM(proj_weight.shape, BF16),
            pltpu.SemaphoreType.DMA((4,)),
        ],
        compiler_params=pltpu.CompilerParams(vmem_limit_bytes=63 * 1024 * 1024),
        name="hand_over",
    )(*grads)


def solution(mesh):
    return jax.shard_map(
        shards,
        mesh=mesh,
        in_specs=(
            P("dp", "tensor"),
            P("tensor"),
            P("dp", "tensor"),
            P("dp", "tensor"),
            P("dp", "tensor"),
            P("dp", "tensor"),
            P("dp", "tensor"),
        ),
        out_specs=(P("dp", "tensor"), P("dp", "tensor")),
        check_vma=False,
    )
```

```python
import jax
import jax.numpy as jnp
from jax import lax
from jax.experimental import pallas as pl
from jax.experimental.pallas import tpu as pltpu
from jax.sharding import PartitionSpec as P

MHEAD = 64
EPSILON = 1e-05
MESH = pl.DeviceIdType.MESH
F32 = jnp.float32
BF16 = jnp.bfloat16
HIGHEST = lax.Precision.HIGHEST


def device(za, zb, yh, x, yl, c):
    return {"dp": (za * 2 + zb) * 4 + yh, "tensor": x * 4 + yl * 2 + c}


def nt_dot(a, b, precision=None):
    return lax.dot_general(
        a, b, (((1,), (1,)), ((), ())), preferred_element_type=F32, precision=precision
    )


def nn_dot(a, b, precision=None):
    return lax.dot_general(
        a, b, (((1,), (0,)), ((), ())), preferred_element_type=F32, precision=precision
    )


class Slots:
    def __init__(self):
        self.count = 0

    def take(self, n):
        first = self.count
        self.count += n
        return first


SLOTS = Slots()
S_HID = SLOTS.take(4)
S_HAG = SLOTS.take(14)
S_W = SLOTS.take(7)
S_SQ = SLOTS.take(8)
S_INV = SLOTS.take(8)
S_GRAM = SLOTS.take(1)
S_DY = SLOTS.take(4)
S_DZ = SLOTS.take(4)
S_DC = SLOTS.take(8)
S_P = SLOTS.take(14)
S_Q = SLOTS.take(4)
S_G = SLOTS.take(3)
S_GIN = SLOTS.take(4)
S_GON = SLOTS.take(4)
S_DOT = SLOTS.take(8)
S_MEAN = SLOTS.take(8)
N_SLOTS = SLOTS.count


def kernel(
    hid_hbm,
    gain_hbm,
    w_hbm,
    bc_hbm,
    x_hbm,
    dy_hbm,
    ld_hbm,
    igrad_hbm,
    wgrad_hbm,
    igrad_ref,
    wgrad_ref,
    hid_ref,
    gain_ref,
    w_ref,
    bc_ref,
    x_ref,
    dy_ref,
    ld_ref,
    ht,
    hall,
    hscaled,
    wall,
    sums,
    sums_in,
    inv,
    dots,
    dots_in,
    gram,
    dall,
    psend,
    precv,
    rsum,
    qrecv,
    gsend,
    grecv,
    grelay,
    prelay,
    ssem,
    rsem,
    lsem,
    isem,
):
    loads = [
        pltpu.make_async_copy(src, dst, isem.at[n])
        for n, (src, dst) in enumerate(
            (
                (hid_hbm, hid_ref),
                (gain_hbm, gain_ref),
                (w_hbm, w_ref),
                (ld_hbm, ld_ref),
                (x_hbm, x_ref),
                (dy_hbm, dy_ref),
                (bc_hbm, bc_ref),
            )
        )
    ]
    for load in loads:
        load.start()

    dp = lax.axis_index("dp")
    ten = lax.axis_index("tensor")
    z, yh = dp // 4, dp % 4
    za, zb = z // 2, z % 2
    x, yl, c = ten // 4, (ten // 2) % 2, ten % 2

    def remote(src, dst, slot, dev, rslot=None):
        rslot = slot if rslot is None else rslot
        return pltpu.make_async_remote_copy(
            src_ref=src,
            dst_ref=dst,
            send_sem=ssem.at[slot],
            recv_sem=rsem.at[rslot],
            device_id=device(*dev),
            device_id_type=MESH,
        )

    sibling = (za, zb, yh, x, yl, 1 - c)
    plane = [(1, 0), (3, 0), (2, 0), (0, 1), (1, 1), (3, 1), (2, 1)]
    column = [(0, 1), (0, 3), (0, 2), (1, 0), (1, 1), (1, 3), (1, 2)]
    depth = [(dza, fc) for dza in (1, 3) for fc in range(2)] + [(0, 1)]

    def plane_dev(dx, fy):
        return (za, zb, yh, (x + dx) % 4, (yl + fy) % 2, c)

    def plane_src(dx, fy):
        return (x + 4 - dx) % 4, (yl + fy) % 2

    def column_dev(k, dy):
        return (za, (zb + k) % 2, (yh + dy) % 4, x, yl, c)

    def far(dza, fc):
        return ((za + dza) % 4, zb, yh, x, yl, (c + fc) % 2)

    def seq(side, y):
        return (y % 2, side, y // 2)

    def hid_target(i, h):
        return (za, yl, 2 * c + i, x, yh % 2, h)

    def hid_target_is_me(i, h):
        return (yl == zb) & (yh == 2 * c + i) & (yl == yh % 2) & (c == h)

    def hid_source(side, u):
        return (za, side, yl + 2 * u, x, zb, yh // 2)

    def hid_source_is_me(side, u):
        return (side == zb) & (yl + 2 * u == yh) & (yl == zb) & (c == yh // 2)

    barrier = pltpu.get_barrier_semaphore()

    def greet(dev):
        pl.semaphore_signal(barrier, inc=1, device_id=device(*dev), device_id_type=MESH)

    greet(sibling)
    for dx, fy in plane:
        greet(plane_dev(dx, fy))
    for k, dy in column:
        greet(column_dev(k, dy))
    for dza, fc in depth[:-1]:
        greet(far(dza, fc))
    met = 8 + 7 + 4
    for i in range(2):
        for h in range(2):

            @pl.when(jnp.logical_not(hid_target_is_me(i, h)))
            def _():
                greet(hid_target(i, h))

    for side in range(2):
        for u in range(2):

            @pl.when(jnp.logical_not(hid_source_is_me(side, u)))
            def _():
                greet(hid_source(side, u))

    own_hop = jnp.where((yl == zb) & (yl == yh % 2) & (c == yh // 2), 1, 0)

    for load in loads[:3]:
        load.wait()
    hid = hid_ref[...].astype(F32)
    gain = gain_ref[...].astype(F32).reshape(1, -1)
    scaled = hid * gain
    for k in range(4):
        ht[k] = scaled[:, k * 128 : (k + 1) * 128].T.astype(BF16)

    def row_of(column):
        return jnp.broadcast_to(column, (128, 128)).T[0:1, :]

    def column_of(row):
        return jnp.broadcast_to(row[0:1, :], (128, 128)).T

    sums[0] = row_of(jnp.sum(hid * hid, axis=1, keepdims=True))
    wall[c, za] = w_ref[pl.ds(pl.multiple_of(c * 128, 128), 128), :]

    pl.semaphore_wait(barrier, met + 8 - 2 * own_hop)

    sq_sibling = remote(sums.at[0], sums_in.at[0, 0], S_SQ, sibling)
    sq_sibling.start()

    def sq_copy(n):
        return remote(sums.at[1], sums_in.at[0, 1 + n], S_SQ + 1 + n, plane_dev(*plane[n]))

    mean_sibling = remote(sums.at[2], sums_in.at[1, 0], S_MEAN, sibling)

    def mean_copy(n):
        return remote(sums.at[3], sums_in.at[1, 1 + n], S_MEAN + 1 + n, plane_dev(*plane[n]))

    def hid_copy(i, h):
        lane = (2 * zb + yh // 2) * 128
        return remote(
            ht.at[2 * i + h],
            hall.at[yh % 2, x, :, pl.ds(pl.multiple_of(lane, 128), 128)],
            S_HID + 2 * i + h,
            hid_target(i, h),
            S_HID + 2 * zb + yh // 2,
        )

    def hid_arrival(side, u):
        lane = (2 * side + u) * 128
        return remote(
            ht.at[0],
            hall.at[yl, x, :, pl.ds(pl.multiple_of(lane, 128), 128)],
            S_HID + 2 * side + u,
            sibling,
        )

    for i in range(2):
        for h in range(2):

            @pl.when(jnp.logical_not(hid_target_is_me(i, h)))
            def _():
                hid_copy(i, h).start()

            @pl.when(hid_target_is_me(i, h))
            def _():
                lane = (2 * zb + yh // 2) * 128
                own = pltpu.make_async_copy(
                    ht.at[2 * i + h],
                    hall.at[yl, x, :, pl.ds(pl.multiple_of(lane, 128), 128)],
                    lsem,
                )
                own.start()
                own.wait()

    def w_copy(n):
        dza, fc = depth[n]
        core = (c + fc) % 2
        return remote(
            w_ref.at[pl.ds(pl.multiple_of(core * 128, 128), 128), :],
            wall.at[c, za],
            S_W + n,
            far(dza, fc),
        )

    def w_arrival(n):
        dza, fc = depth[n]
        return remote(
            w_ref.at[0:128, :], wall.at[(c + fc) % 2, (za + 4 - dza) % 4], S_W + n, sibling
        )

    for n in range(5):
        w_copy(n).start()

    def w_on(j):
        block = wall.at[j, (za + (1, 3)[j] + 2) % 4]
        return remote(block, block, S_W + 5 + j, far((1, 3)[j], 0))

    def w_on_arrival(j):
        block = wall.at[j, (za + 2) % 4]
        return remote(block, block, S_W + 5 + j, sibling)

    for load in loads[3:]:
        load.wait()
    rows = lax.broadcasted_iota(jnp.int32, (128, 128), 0)
    cols = lax.broadcasted_iota(jnp.int32, (128, 128), 1)
    causal = rows >= cols
    heads = ld_ref.shape[0]
    padded = jnp.concatenate([ld_ref[...], jnp.zeros((128 - heads, 128), F32)], axis=0)
    running_t = nt_dot(padded, causal.astype(F32), HIGHEST)
    running = running_t.T
    low = cols < MHEAD
    total = jnp.zeros((128, 128), F32)
    for p in range(heads // 2):
        xp = x_ref[:, p * 128 : (p + 1) * 128]
        zero = jnp.zeros_like(xp)
        both = jnp.concatenate([jnp.where(low, xp, zero), jnp.where(low, zero, xp)], axis=0)
        inner = nt_dot(dy_ref[:, p * 128 : (p + 1) * 128], both)
        for k in range(2):
            h = 2 * p + k
            gap = running[:, h : h + 1] - running_t[h : h + 1, :]
            decay = jnp.exp(jnp.where(causal, gap, -1e30))
            total = total + inner[:, k * 128 : (k + 1) * 128] * decay
    gram[0] = total

    gram_copy = remote(gram.at[0], gram.at[1], S_GRAM, sibling)
    gram_copy.start()

    sq_sibling.wait_recv()
    sums[1] = sums[0] + sums_in[0, 0]
    for n in range(7):
        sq_copy(n).start()

    gram_copy.wait_recv()
    total = gram[0] + gram[1]
    bc = bc_ref[...].astype(F32)
    grad_b = nn_dot(total.T, bc[:, 128:], HIGHEST)
    grad_c = nn_dot(total, bc[:, :128], HIGHEST)
    dall[(c,) + seq(zb, yh)] = jnp.concatenate([grad_b, grad_c], axis=1).astype(BF16)

    def d_y(dy):
        block = dall.at[(c,) + seq(zb, yh)]
        return remote(block, block, S_DY + dy, column_dev(0, dy))

    def d_far(dy):
        half = slice(0, 64) if dy == 1 else slice(64, 128)
        block = dall.at[(c,) + seq(zb, (yh + 4 - dy) % 4) + (half,)]
        return remote(block, block, S_DY + dy - 1, column_dev(0, dy))

    def d_far_arrival(dy):
        half = slice(0, 64) if dy == 1 else slice(64, 128)
        block = dall.at[(c,) + seq(zb, (yh + 2) % 4) + (half,)]
        return remote(block, block, S_DY + dy - 1, sibling)

    def d_y_arrival(dy):
        block = dall.at[(c,) + seq(zb, (yh + 4 - dy) % 4)]
        return remote(block, block, S_DY + dy, sibling)

    def d_z(dy):
        if dy == 2:
            block = dall.at[(c,) + seq(1 - zb, yh)]
            return remote(block, block, S_DZ + dy, column_dev(0, 2))
        block = dall.at[(c,) + seq(zb, (yh + 4 - dy) % 4)]
        return remote(block, block, S_DZ + dy, column_dev(1, 0))

    def d_z_arrival(dy):
        block = dall.at[(c,) + seq(1 - zb, (yh + 4 - dy) % 4)]
        return remote(block, block, S_DZ + dy, sibling)

    def d_c(k, dy):
        block = dall.at[(c,) + seq((zb + k) % 2, (yh + 4 - dy) % 4)]
        return remote(block, block, S_DC + 4 * k + dy, sibling)

    def d_c_arrival(k, dy):
        block = dall.at[(1 - c,) + seq((zb + k) % 2, (yh + 4 - dy) % 4)]
        return remote(block, block, S_DC + 4 * k + dy, sibling)

    for dy in (1, 3):
        d_y(dy).start()
    d_z(0).start()
    d_c(0, 0).start()

    def h_block(k, sy, sx):
        lane = ((zb + k) % 2) * 256
        return hall.at[sy, sx, :, pl.ds(pl.multiple_of(lane, 128), 256)]

    def h_copy(k, n):
        dx, fy = plane[n]
        block = h_block(k, (yl + fy) % 2 if dx else yl, x)
        dev = (za, zb, yh, (x + dx) % 4, yl if dx else 1 - yl, c)
        return remote(block, block, S_HAG + 7 * k + n, dev)

    def h_arrival(k, n):
        sx, sy = plane_src(*plane[n])
        block = h_block(k, sy, sx)
        return remote(block, block, S_HAG + 7 * k + n, sibling)

    def hid_on(k):
        side = (zb + k) % 2
        for u in range(2):

            @pl.when(jnp.logical_not(hid_source_is_me(side, u)))
            def _():
                hid_arrival(side, u).wait_recv()

        for n in (3, 0, 1):
            h_copy(k, n).start()

    def hid_across(k):
        h_arrival(k, 3).wait_recv()
        for n in (4, 5):
            h_copy(k, n).start()

    def hid_far(k, fy):
        sx, sy = plane_src((1, 3)[k], fy)
        block = h_block(k, sy, sx)
        slot = S_HAG + 7 * k + 2 + 4 * fy
        return remote(block, block, slot, (za, zb, yh, (x + (1, 3)[k]) % 4, yl, c))

    def hid_relay(k, fy):
        h_arrival(k, k + 4 * fy).wait_recv()
        hid_far(k, fy).start()

    hid_on(0)
    hid_on(1)

    def d_on(dy):
        if dy == 2:
            d_far_arrival(1).wait_recv()
            d_far_arrival(3).wait_recv()
        else:
            d_y_arrival(dy).wait_recv()
            d_far(dy).start()
            d_z(dy).start()
        d_c(0, dy).start()

    square = sums[1]
    for n in range(7):
        sq_copy(n).wait_recv()
        square = square + sums_in[0, 1 + n]
    mean_square = square * (1.0 / 8192.0) + EPSILON
    inv_root = lax.rsqrt(mean_square)
    inv[seq(zb, yh)] = inv_root

    def inv_copy(n):
        block = inv.at[seq(zb, yh)]
        return remote(block, block, S_INV + n, column_dev(*column[n]))

    def inv_arrival(n):
        k, dy = column[n]
        block = inv.at[seq((zb + k) % 2, (yh + 4 - dy) % 4)]
        return remote(block, block, S_INV + n, sibling)

    for n in range(7):
        inv_copy(n).start()

    d_on(1)
    d_on(3)
    for n in range(4):
        w_arrival(n).wait_recv()
    for j in range(2):
        w_on(j).start()
    d_z_arrival(0).wait_recv()
    d_z(2).start()
    d_c(1, 0).start()
    hid_across(0)
    hid_relay(0, 0)
    hid_relay(1, 0)
    hid_across(1)

    d_on(2)
    for dy in (0, 1, 3, 2):
        d_c_arrival(0, dy).wait_recv()

    def p_copy(k, n):
        dx, fy = plane[n]
        side = (zb + k) % 2
        relayed = k == 0 and (dx, fy) in ((1, 0), (3, 1))
        return remote(
            prelay.at[fy] if relayed else psend.at[side, (yl + fy) % 2, (x + dx) % 4],
            precv.at[side, yl, x],
            S_P + 7 * k + n,
            plane_dev(dx, fy),
        )

    def p_arrival(k, n):
        sx, sy = plane_src(*plane[n])
        block = precv.at[(zb + k) % 2, sy, sx]
        return remote(block, block, S_P + 7 * k + n, sibling)

    def terms(k, dza):
        side, tx = (zb + k) % 2, (za + dza) % 4
        for py in range(2):
            out = nt_dot(dall[0, py, side].reshape(256, 256), wall[0, tx])
            out = out + nt_dot(dall[1, py, side].reshape(256, 256), wall[1, tx])
            psend[side, py, tx] = out.astype(BF16)

    def p_far(fy):
        block = psend.at[zb, (yl + fy) % 2, (x + 2) % 4]
        dev = (za, zb, yh, (x + (1, 3)[fy]) % 4, yl, c)
        return remote(block, prelay.at[fy], S_P + 2 + 4 * fy, dev)

    def p_relay(fy):
        p_far(fy).wait_recv()
        to = (yl + fy) % 2, (x + (1, 3)[fy]) % 4
        own = psend[(zb,) + to].astype(F32)
        prelay[fy] = (own + prelay[fy].astype(F32)).astype(BF16)
        p_copy(0, 5 * fy).start()

    def p_start(k, dza):
        for n, (dx, fy) in enumerate(plane):
            if (dx, fy) in ((1, 0), (3, 1)):
                continue

            @pl.when((x + dx) % 4 == (za + dza) % 4)
            def _():
                if dx == 2:
                    p_far(fy).start()
                else:
                    p_copy(k, n).start()

    w_arrival(4).wait_recv()
    for dza in (0, 1, 3):
        terms(0, dza)
    hid_relay(0, 1)
    hid_relay(1, 1)
    for dza in (0, 1, 3):
        p_start(0, dza)
    for j in range(2):
        w_on_arrival(j).wait_recv()
    terms(0, 2)
    p_start(0, 2)
    for dy in (1, 3, 2):
        d_z_arrival(dy).wait_recv()
        d_c(1, dy).start()
    for dy in (0, 1, 3, 2):
        d_c_arrival(1, dy).wait_recv()
    for dza in range(4):
        terms(1, dza)

    def g_dev(dza, j):
        return ((za + dza) % 4, zb, yh, x, yl, j)

    def g_copy(j):
        dza = (3, 1)[j]
        return remote(
            gsend.at[(za + dza) % 4, j], grecv.at[za, c], S_G + j, g_dev(dza, j), S_G + c
        )

    def g_arrival(h):
        block = grecv.at[jnp.where(c == 0, (za + 1) % 4, (za + 3) % 4), h]
        return remote(block, block, S_G + h, sibling)

    def g_sibling():
        return remote(gsend.at[za, 1 - c], grecv.at[za, c], S_G + 2, sibling)

    def g_relay(j, part):
        half = slice(part * 64, part * 64 + 64)
        return remote(
            gsend.at[(za + 2) % 4, j, half],
            grelay.at[j, half],
            S_GIN + 2 * j + part,
            g_dev((1, 3)[j], c),
        )

    def g_on(j, part):
        dza = (1, 3)[j]
        half = slice(part * 64, part * 64 + 64)
        return remote(
            gsend.at[(za + dza) % 4, j, half],
            grecv.at[za, c, half],
            S_GON + 2 * j + part,
            g_dev(dza, j),
            S_GON + 2 * c + part,
        )

    def g_on_arrival(h, part):
        half = slice(part * 64, part * 64 + 64)
        block = grecv.at[jnp.where(c == 0, (za + 3) % 4, (za + 1) % 4), h, half]
        return remote(block, block, S_GON + 2 * h + part, sibling)

    for n in range(7):
        inv_arrival(n).wait_recv()
    inv_rows = [
        jnp.concatenate([inv[sy, side, u][0:1, :] for side in range(2) for u in range(2)], axis=1)
        for sy in range(2)
    ]
    inv_rows = [inv_rows[sy] * (1.0 / 64.0) for sy in range(2)]
    own_inv = jnp.where(yl == 0, inv_rows[0], inv_rows[1])
    other_inv = jnp.where(yl == 0, inv_rows[1], inv_rows[0])

    def scale(dx, fy):
        sx, sy = plane_src(dx, fy)
        row = other_inv if fy else own_inv
        hscaled[sy, sx] = (hall[sy, sx].astype(F32) * row).astype(BF16)

    scale(0, 0)
    scale(0, 1)
    for n in (0, 1, 4, 5, 2, 6):
        for k in range(2):
            if n % 4 != k:
                h_arrival(k, n).wait_recv()
        scale(*plane[n])
    eye = (rows == cols).astype(F32)
    for py in range(2):
        for side in range(2):
            for u in range(2):
                part = slice(u * 128, (u + 1) * 128)
                lane = (2 * side + u) * 128
                prod = jnp.zeros((128, 128), F32)
                for f in range(4):
                    prod = prod + nn_dot(
                        psend[side, py, f, part, :], hall[py, f, :, lane : lane + 128]
                    )
                row = jnp.sum(prod * eye, axis=0, keepdims=True)
                dots[py, side, u] = row

    def dot_copy(n):
        k, dy = column[n]
        block = dots.at[seq((zb + k) % 2, (yh + dy) % 4)]
        return remote(block, dots_in.at[n], S_DOT + n, column_dev(k, dy))

    for n in range(7):
        dot_copy(n).start()
    def g_terms(first, count, j):
        rows = [hscaled[sy, pl.ds(first, count)].reshape(count * 128, 512) for sy in range(2)]
        out = nn_dot(rows[0], dall[j, 0].reshape(512, 256))
        out = out + nn_dot(rows[1], dall[j, 1].reshape(512, 256))
        gsend[pl.ds(first, count), j] = out.astype(BF16).reshape(count, 128, 256)

    for j in range(2):
        g_terms((za + 2) % 4, 1, j)
        g_relay(j, 0).start()
    for j in range(2):
        g_relay(j, 1).start()
    p_relay(0)
    p_relay(1)
    for n in range(7):
        p_copy(1, n).start()

    for j in range(2):
        g_terms((za + (3, 1)[j]) % 4, 1, j)
        g_copy(j).start()
    for j in range(2):
        g_terms((za + (1, 3)[j]) % 4, 1, j)
        g_terms(za, 1, j)
    g_sibling().start()

    def q_copy(k, u):
        side = (zb + k) % 2
        return remote(
            rsum.at[side, u],
            qrecv.at[yh % 2, c],
            S_Q + 2 * k + u,
            hid_source(side, u),
            S_Q + 2 * (yh % 2) + c,
        )

    def owners(k):
        side = (zb + k) % 2
        arrivals = (1, 4, 3, 0, 5) if k == 0 else range(7)
        for n in arrivals:
            p_arrival(k, n).wait_recv()
        acc = psend[side, yl, x].astype(F32)
        for n in arrivals:
            sx, sy = plane_src(*plane[n])
            acc = acc + precv[side, sy, sx].astype(F32)
        rsum[side] = acc.astype(BF16).reshape(2, 128, 128)
        for u in range(2):

            @pl.when(jnp.logical_not(hid_source_is_me(side, u)))
            def _():
                q_copy(k, u).start()

            @pl.when(hid_source_is_me(side, u))
            def _():
                own = pltpu.make_async_copy(rsum.at[side, u], qrecv.at[yh % 2, c], lsem)
                own.start()
                own.wait()

    def g_relays(part):
        half = slice(part * 64, part * 64 + 64)
        for j in range(2):
            g_relay(j, part).wait_recv()
            to = (za + (1, 3)[j]) % 4
            own = gsend[to, j, half].astype(F32)
            gsend[to, j, half] = (own + grelay[j, half].astype(F32)).astype(BF16)
            g_on(j, part).start()

    g_relays(0)
    for n in range(7):
        dot_copy(n).wait_recv()
    value = dots[seq(zb, yh)]
    for n in range(7):
        value = value + dots_in[n]
    sums[2] = value
    mean_sibling.start()
    g_relays(1)
    mean_sibling.wait_recv()
    sums[3] = sums[2] + sums_in[1, 0]
    for n in range(7):
        mean_copy(n).start()

    owners(0)
    owners(1)

    g_sibling().wait_recv()
    for h in range(2):
        g_arrival(h).wait_recv()
        for part in range(2):
            g_on_arrival(h, part).wait_recv()
    grecv[za, c] = gsend[za, c]
    for h in range(2):
        acc = grecv[za, h].astype(F32)
        for d in range(2):
            acc = acc + grecv[(za + (3, 1)[d]) % 4, h].astype(F32)
        wgrad_ref[h * 128 : (h + 1) * 128, :] = acc.astype(BF16)

    wgrad_out = pltpu.make_async_copy(wgrad_ref, wgrad_hbm, isem.at[7])
    wgrad_out.start()
    dot = sums[3]
    for n in range(7):
        mean_copy(n).wait_recv()
        dot = dot + sums_in[1, 1 + n]
    factor = column_of(dot * (1.0 / 8192.0) / mean_square)
    inv_column = column_of(inv_root)
    for i in range(2):
        for h in range(2):

            @pl.when(jnp.logical_not(hid_target_is_me(i, h)))
            def _():
                remote(rsum.at[0, 0], qrecv.at[i, h], S_Q + 2 * i + h, sibling).wait_recv()

    for i in range(2):
        for h in range(2):
            k = 2 * i + h
            part = slice(k * 128, (k + 1) * 128)
            grad = qrecv[i, h].astype(F32) * gain[:, part]
            igrad_ref[:, part] = ((grad - hid[:, part] * factor) * inv_column).astype(BF16)

    igrad_out = pltpu.make_async_copy(igrad_ref, igrad_hbm, isem.at[8])
    igrad_out.start()

    for i in range(2):
        for h in range(2):

            @pl.when(jnp.logical_not(hid_target_is_me(i, h)))
            def _():
                hid_copy(i, h).wait_send()

    for k in range(2):
        for u in range(2):

            @pl.when(jnp.logical_not(hid_source_is_me((zb + k) % 2, u)))
            def _():
                q_copy(k, u).wait_send()

    sq_sibling.wait_send()
    for n in range(7):
        sq_copy(n).wait_send()
        mean_copy(n).wait_send()
    mean_sibling.wait_send()
    gram_copy.wait_send()
    for n in range(5):
        w_copy(n).wait_send()
    g_sibling().wait_send()
    for j in range(2):
        w_on(j).wait_send()
        g_copy(j).wait_send()
        for part in range(2):
            g_relay(j, part).wait_send()
            g_on(j, part).wait_send()
    for n in range(7):
        for k in range(2):
            if n % 4 != 2:
                h_copy(k, n).wait_send()
            else:
                hid_far(k, n // 4).wait_send()
        if n % 4 != 2:
            p_copy(0, n).wait_send()
        else:
            p_far(n // 4).wait_send()
        p_copy(1, n).wait_send()
        inv_copy(n).wait_send()
        dot_copy(n).wait_send()
    for dy in range(4):
        if dy % 2:
            d_y(dy).wait_send()
            d_far(dy).wait_send()
        d_z(dy).wait_send()
        d_c(0, dy).wait_send()
        d_c(1, dy).wait_send()
    wgrad_out.wait()
    igrad_out.wait()


def hand_over(igrad_ref, wgrad_ref, igrad_out, wgrad_out, igrad, wgrad, sem):
    ins = [
        pltpu.make_async_copy(igrad_ref, igrad, sem.at[0]),
        pltpu.make_async_copy(wgrad_ref, wgrad, sem.at[1]),
    ]
    outs = [
        pltpu.make_async_copy(igrad, igrad_out, sem.at[2]),
        pltpu.make_async_copy(wgrad, wgrad_out, sem.at[3]),
    ]
    for copy in ins:
        copy.start()
    for first, second in zip(ins, outs):
        first.wait()
        second.start()
    for copy in outs:
        copy.wait()


def shards(hidden, gain, proj_weight, b_c, ssm_x, dy, log_decay):
    hbm = pl.BlockSpec(memory_space=pl.ANY)
    grads = pl.pallas_call(
        kernel,
        out_shape=(
            jax.ShapeDtypeStruct(hidden.shape, BF16),
            jax.ShapeDtypeStruct(proj_weight.shape, BF16),
        ),
        in_specs=[hbm] * 7,
        out_specs=(hbm, hbm),
        scratch_shapes=[
            pltpu.VMEM(hidden.shape, BF16),
            pltpu.VMEM(proj_weight.shape, BF16),
            pltpu.VMEM(hidden.shape, BF16),
            pltpu.VMEM(gain.shape, BF16),
            pltpu.VMEM(proj_weight.shape, BF16),
            pltpu.VMEM(b_c.shape, BF16),
            pltpu.VMEM(ssm_x.shape, BF16),
            pltpu.VMEM(dy.shape, BF16),
            pltpu.VMEM(log_decay.shape[::-1], F32),
            pltpu.VMEM((4, 128, 128), BF16),
            pltpu.VMEM((2, 4, 128, 512), BF16),
            pltpu.VMEM((2, 4, 128, 512), BF16),
            pltpu.VMEM((2, 4, 128, 256), BF16),
            pltpu.VMEM((4, 1, 128), F32),
            pltpu.VMEM((2, 8, 1, 128), F32),
            pltpu.VMEM((2, 2, 2, 1, 128), F32),
            pltpu.VMEM((2, 2, 2, 1, 128), F32),
            pltpu.VMEM((7, 1, 128), F32),
            pltpu.VMEM((2, 128, 128), F32),
            pltpu.VMEM((2, 2, 2, 2, 128, 256), BF16),
            pltpu.VMEM((2, 2, 4, 256, 128), BF16),
            pltpu.VMEM((2, 2, 4, 256, 128), BF16),
            pltpu.VMEM((2, 2, 128, 128), BF16),
            pltpu.VMEM((2, 2, 128, 128), BF16),
            pltpu.VMEM((4, 2, 128, 256), BF16),
            pltpu.VMEM((4, 2, 128, 256), BF16),
            pltpu.VMEM((2, 128, 256), BF16),
            pltpu.VMEM((2, 256, 128), BF16),
            pltpu.SemaphoreType.DMA((N_SLOTS,)),
            pltpu.SemaphoreType.DMA((N_SLOTS,)),
            pltpu.SemaphoreType.DMA,
            pltpu.SemaphoreType.DMA((9,)),
        ],
        compiler_params=pltpu.CompilerParams(
            collective_id=0, has_side_effects=True, vmem_limit_bytes=63 * 1024 * 1024
        ),
        name="projection_backward",
    )(hidden, gain, proj_weight, b_c, ssm_x, dy, log_decay.T)
    return pl.pallas_call(
        hand_over,
        out_shape=tuple(jax.ShapeDtypeStruct(grad.shape, grad.dtype) for grad in grads),
        in_specs=[hbm] * 2,
        out_specs=(hbm, hbm),
        scratch_shapes=[
            pltpu.VMEM(hidden.shape, BF16),
            pltpu.VMEM(proj_weight.shape, BF16),
            pltpu.SemaphoreType.DMA((4,)),
        ],
        compiler_params=pltpu.CompilerParams(vmem_limit_bytes=63 * 1024 * 1024),
        name="hand_over",
    )(*grads)


def solution(mesh):
    return jax.shard_map(
        shards,
        mesh=mesh,
        in_specs=(
            P("dp", "tensor"),
            P("tensor"),
            P("dp", "tensor"),
            P("dp", "tensor"),
            P("dp", "tensor"),
            P("dp", "tensor"),
            P("dp", "tensor"),
        ),
        out_specs=(P("dp", "tensor"), P("dp", "tensor")),
        check_vma=False,
    )
```
